256 devices in a mesh: ctx: 64 (over z, y, x_lo), tp: 4 (over x_hi, core).
Axes of the slice: x: 4 (x_hi: 2, x_lo: 2; x = x_hi * 2 + x_lo), y: 4, z: 8, core: 2. Of those that a mesh axis runs over, the one named last changes fastest.
Arguments:
- block_input: bfloat16 [8192, 4096], P(('ctx', 'tp')), may hold values from -6 to 6
- featurizer: bfloat16 [4096, 3, 2048], P('ctx', None, 'tp'), may hold values from -0.09375 to 0.09375
- filters: bfloat16 [2048, 128], P('tp'), may hold values from -0.5 to 0.5
- out_weight: bfloat16 [4096, 2048], P('ctx', 'tp'), may hold values from -0.125 to 0.125
- grad_output: bfloat16 [8192, 4096], P(('ctx', 'tp')), may hold values from -24 to 24
Outputs:
- grad_features: bfloat16 [8192, 3, 2048], P('ctx', None, 'tp')
- grad_out_weight: float32 [4096, 2048], P('ctx', 'tp')
- grad_filters: float32 [2048, 128], P('tp')
The draws below stay inside these ranges and needn't reach their ends.
All inputs are finite; a program needn't handle non-finite values.
Results may differ from the reference program's by a relative error of at most 0.015.
Values may be sent and summed in bfloat16 or wider, within the bound.
A program may use at most 128 MiB of HBM per device.

```python
import math
import jax
import jax.numpy as jnp
from jax import lax

D = 4096
HC = 2048
TAPS = 128
LENGTH = 8192


def strengthened(values, rng, source, target, shards_of, factor):
    owner, partner = [(jnp.arange(values.shape[position]) // (values.shape[position] // shards_of)).reshape([-1 if axis == position else 1 for axis in range(values.ndim)]) for position in (source, target)]
    chosen = jax.random.permutation(rng, shards_of)[partner]
    strong = (owner == chosen) | (owner == (partner + shards_of // 2) % shards_of)
    return jnp.where(strong, factor * values, values)


def block_levels(rng, dims, pieces, low, largest):
    factor_of, own = 1.0, jax.random.fold_in(rng, 6)
    for dim, shards_of in pieces:
        steps = jnp.exp(jax.random.uniform(jax.random.fold_in(own, dim), (shards_of,), jnp.float32, low / len(pieces), largest / len(pieces)))
        factor_of = factor_of * jnp.repeat(steps, dims[dim] // shards_of).reshape([-1 if axis == dim else 1 for axis in range(len(dims))])
    return factor_of


def centred(key, extent, scale, limit, pieces=(), kind=jnp.bfloat16):
    level = block_levels(key, extent, pieces, -0.22, 0.18) if pieces else 1.0
    array = jax.random.normal(key, extent, jnp.float32) * scale * level
    return jnp.minimum(jnp.maximum(array, -limit), limit).astype(kind)


def heavy_noise(own_key, extent, scale, most, shards, heavy, kind=jnp.bfloat16):
    values = scale * jax.random.normal(own_key, extent, jnp.float32)
    if shards:
        values = values * block_levels(own_key, extent, shards, -0.22, 0.18)
    return jnp.clip(strengthened(values, jax.random.fold_in(own_key, 3), *heavy), -most, most).astype(kind)


def setup_inputs(seed: int = 0) -> dict:
    seeds = jax.random.split(jax.random.key(seed), 6)
    return {
        "block_input": centred(seeds[0], (LENGTH, D), 1.0, 6.0, ((0, 256),)),
        "featurizer": centred(seeds[1], (D, 3, HC), D ** -0.5, 0.09375, ((0, 64), (2, 4))),
        "filters": centred(seeds[2], (HC, TAPS), TAPS ** -0.5, 0.5, ((0, 4),)),
        "out_weight": centred(seeds[3], (D, HC), HC ** -0.5, 0.125, ((0, 64), (1, 4))),
        "grad_output": heavy_noise(seeds[4], (LENGTH, D), 1.0, 24.0, ((0, 256),), (0, 1, 256, 6.0)),
    }


def skew_taps(taps_float):
    width_group, ntaps = taps_float.shape
    zero_first = jnp.zeros((width_group, 1), taps_float.dtype)
    zero_rest = jnp.zeros((width_group, ntaps), taps_float.dtype)
    base_row = jnp.concatenate([zero_first, taps_float[:, ::-1], zero_rest], axis=1)
    tiled = jnp.broadcast_to(base_row[:, None, :], (width_group, ntaps, 2 * ntaps + 1))
    flat = tiled.reshape(width_group, ntaps * (2 * ntaps + 1))[:, :2 * ntaps * ntaps]
    return flat.reshape(width_group, ntaps, 2 * ntaps)

def block_windows(extended, ntaps):
    count_blocks = extended.shape[0] // ntaps - 1
    blocks = extended.reshape(count_blocks + 1, ntaps, extended.shape[1])
    return jnp.concatenate([blocks[:-1], blocks[1:]], axis=1)

def causal_conv(signal, taps_float):
    length, channels = signal.shape
    ntaps = taps_float.shape[1]
    group = min(128, channels)
    ngroups = channels // group
    signal_groups = signal.reshape(length, ngroups, group).transpose(1, 0, 2)
    tap_groups = taps_float.reshape(ngroups, group, ntaps)

    def one_group(group_pair):
        signal_part, taps_part = group_pair
        extended = jnp.concatenate([jnp.zeros((ntaps, group), signal_part.dtype), signal_part], axis=0)
        windows = block_windows(extended, ntaps)
        result = jnp.einsum('ciw,bwc->bic', skew_taps(taps_part), windows)
        return result.reshape(length, group)
    outputs = lax.map(one_group, (signal_groups, tap_groups))
    return outputs.transpose(1, 0, 2).reshape(length, channels)

def reference(block_input, featurizer, filters, out_weight, grad_output):
    length = block_input.shape[0]
    width = featurizer.shape[2]
    ntaps = filters.shape[1]
    flat_weight = featurizer.reshape(block_input.shape[1], 3 * width)
    features = jnp.dot(block_input, flat_weight, preferred_element_type=jnp.float32).astype(jnp.bfloat16)
    features = features.reshape(length, 3, width)
    query_rows = features[:, 0].astype(jnp.float32)
    key_rows = features[:, 1].astype(jnp.float32)
    value_rows = features[:, 2].astype(jnp.float32)
    gated = (key_rows * value_rows).astype(jnp.bfloat16)
    taps_float = filters.astype(jnp.float32)
    mixed = causal_conv(gated.astype(jnp.float32), taps_float)
    mixer_out = (query_rows * mixed).astype(jnp.bfloat16)
    grad_mixer = jnp.dot(grad_output, out_weight, preferred_element_type=jnp.float32).astype(jnp.bfloat16)
    scale_factor = 1.0 / math.sqrt(length)
    grad_out_weight = lax.dot_general(grad_output, mixer_out, (((0,), (0,)), ((), ())), preferred_element_type=jnp.float32) * scale_factor
    grad_mixer_f = grad_mixer.astype(jnp.float32)
    grad_mixed = (grad_mixer_f * query_rows).astype(jnp.bfloat16)
    grad_mixed_f = grad_mixed.astype(jnp.float32)
    grad_gated = causal_conv(grad_mixed_f[::-1], taps_float)[::-1]
    grad_features = jnp.stack([grad_mixer_f * mixed, grad_gated * value_rows, grad_gated * key_rows], axis=1).astype(jnp.bfloat16)
    padded = jnp.concatenate([jnp.zeros((ntaps, width), jnp.float32), gated.astype(jnp.float32)], axis=0)

    def one_tap(lag):
        shifted = lax.dynamic_slice_in_dim(padded, ntaps - lag, length, 0)
        return lax.optimization_barrier(jnp.sum(grad_mixed_f * shifted, axis=0))
    grad_filters = lax.map(one_tap, jnp.arange(ntaps, dtype=jnp.int32)).T * scale_factor
    return (grad_features, grad_out_weight, grad_filters)
```

```python
import functools
import math

import jax
import jax.numpy as jnp
from jax import lax
from jax.experimental import pallas as pl
from jax.experimental.pallas import tpu as pltpu
from jax.sharding import PartitionSpec as P

MESH = pl.DeviceIdType.MESH
BF = jnp.bfloat16
F32 = jnp.float32
NZ = 8
RING = 4


def coords():
    ctx = lax.axis_index("ctx")
    tp = lax.axis_index("tp")
    z = ctx // 8
    y = (ctx // 2) % 4
    xl = ctx % 2
    xh = tp // 2
    core = tp % 2
    return xh, xl, y, z, core


def dev(xh, xl, y, z, core):
    return ((z * 4 + y) * 2 + xl, xh * 2 + core)


def devx(x, y, z, core):
    return dev(x // 2, x % 2, y, z, core)


def slot_of(x):
    return (x % 2) * 2 + x // 2


def remote(src, dst, ssem, rsem, device):
    return pltpu.make_async_remote_copy(
        src_ref=src, dst_ref=dst, send_sem=ssem, recv_sem=rsem, device_id=device, device_id_type=MESH
    )


FP, FM, HP, HM = 0, 1, 2, 3


class Plane:
    def __init__(self, own, buf, ssem, rsem, base, here):
        self.own, self.buf, self.ssem, self.rsem, self.base = own, buf, ssem, rsem, base
        self.x, self.y, self.z, self.core = here
        self.sent = []

    def unit(self, lr, a, b, half):
        dx, dy = (a, b) if lr == 0 else (b, a)
        xx = (self.x + dx) % 4
        yy = (self.y + dy) % 4
        cols = pl.ds(0, 4096) if half is None else pl.ds(half * 2048, 2048)
        return self.buf.at[yy, slot_of(xx), pl.ds(lr * 16, 16), cols]

    def neighbour(self, lr, axis, by):
        if (lr == 0) == (axis == 0):
            return devx((self.x + by) % 4, self.y, self.z, self.core)
        return devx(self.x, (self.y + by) % 4, self.z, self.core)

    def sem(self, lr, axis, a, kind):
        return self.base + lr * 20 + (kind if axis == 0 else 4 + a * 4 + kind)

    def send(self, lr, axis, a, kind):
        by = 1 if kind in (FP, HP) else -1
        back = {FP: 0, FM: 0, HP: 3, HM: 1}[kind]
        half = {FP: None, FM: None, HP: 0, HM: 1}[kind]
        place = (back, 0) if axis == 0 else (a, back)
        dst = self.unit(lr, place[0], place[1], half)
        src = self.own.at[pl.ds(lr * 16, 16), :] if place == (0, 0) else dst
        s = self.sem(lr, axis, a, kind)
        copy = remote(src, dst, self.ssem.at[s], self.rsem.at[s], self.neighbour(lr, axis, by + 4 if by < 0 else by))
        copy.start()
        self.sent.append(copy)

    def wait(self, lr, axis, a, kind):
        off = {FP: 3, FM: 1, HP: 2, HM: 2}[kind]
        half = {FP: None, FM: None, HP: 0, HM: 1}[kind]
        place = (off, 0) if axis == 0 else (a, off)
        dst = self.unit(lr, place[0], place[1], half)
        s = self.sem(lr, axis, a, kind)
        remote(dst, dst, self.ssem.at[s], self.rsem.at[s], self.neighbour(lr, axis, 1)).wait_recv()

    def step1(self):
        for lr in range(2):
            for kind in (FP, FM):
                self.send(lr, 0, 0, kind)
        for lr in range(2):
            for kind in (FP, FM):
                self.send(lr, 1, 0, kind)

    def step2(self):
        for kind, a, hkind in ((FP, 3, HP), (FM, 1, HM)):
            for lr in range(2):
                self.wait(lr, 0, 0, kind)
                self.send(lr, 0, 0, hkind)
                self.send(lr, 1, a, FP)
                self.send(lr, 1, a, FM)

    def step3(self):
        for lr in range(2):
            self.wait(lr, 0, 0, HP)
            self.wait(lr, 0, 0, HM)
            self.send(lr, 1, 2, FP)
            self.send(lr, 1, 2, FM)

    def step4(self, a):
        for kind, hkind in ((FP, HP), (FM, HM)):
            for lr in range(2):
                self.wait(lr, 1, a, kind)
                self.send(lr, 1, a, hkind)

    def step5(self):
        for a in (0, 3, 1, 2):
            for lr in range(2):
                self.wait(lr, 1, a, HP)
                self.wait(lr, 1, a, HM)

    def finish(self):
        for copy in self.sent:
            copy.wait_send()


def gather_kernel(
    x_ref, g_ref, fw_ref, filt_ref,
    qkvg_ref, gext_out, mext_out, taps_out, gall_out,
    xbuf, gbuf, wbuf, acc, gext, mext, filt_recv, filt_own,
    psend, precv, wsend, wrecv, hsend, hrecv, lsem,
):
    xh, xl, y, z, core = coords()
    x = xh * 2 + xl
    here = (x, y, z, core)
    other = 1 - core
    zp, zm = (z + 1) % 8, (z + 7) % 8
    partner = dev(xh, xl, y, z, other)

    barrier = pltpu.get_barrier_semaphore()
    greet = [
        devx((x + 1) % 4, y, z, core), devx((x + 3) % 4, y, z, core),
        devx(x, (y + 1) % 4, z, core), devx(x, (y + 3) % 4, z, core),
        devx(x, y, zp, core), devx(x, y, zm, core),
        devx(x, y, zp, other), devx(x, y, zm, other),
        partner,
        dev(xh, 1 - xl, y, z, other),
    ] + [dev(xh, core, (y + dy) % 4, z, xl) for dy in (1, 2, 3)]
    for d in greet:
        pl.semaphore_signal(barrier, inc=1, device_id=d, device_id_type=MESH)
    pl.semaphore_wait(barrier, len(greet))

    xs = Plane(x_ref, xbuf, psend, precv, 0, here)
    gs = Plane(g_ref, gbuf, psend, precv, 40, here)
    sent = []

    for dy in (1, 2, 3):
        yy = (y + dy) % 4
        c = remote(fw_ref.at[yy], wbuf.at[z, y, xl], wsend.at[dy], wrecv.at[dy], dev(xh, core, yy, z, xl))
        c.start()
        sent.append(c)
    same = xl == core
    own_local = pltpu.make_async_copy(fw_ref.at[y], wbuf.at[z, y, core], lsem.at[0])
    own_remote = remote(
        fw_ref.at[y], wbuf.at[z, y, xl], wsend.at[0], wrecv.at[0], dev(xh, 1 - xl, y, z, other)
    )

    @pl.when(same)
    def _():
        own_local.start()

    @pl.when(jnp.logical_not(same))
    def _():
        own_remote.start()

    filt_copy = remote(filt_ref.at[y], filt_recv, hsend.at[0], hrecv.at[0], partner)
    filt_copy.start()
    sent.append(filt_copy)
    filt_local = pltpu.make_async_copy(filt_ref.at[y], filt_own, lsem.at[1])
    filt_local.start()

    xs.step1()
    x_local = pltpu.make_async_copy(x_ref, xbuf.at[y, slot_of(x)], lsem.at[2])
    x_local.start()
    g_local = pltpu.make_async_copy(g_ref, gbuf.at[y, slot_of(x)], lsem.at[3])
    g_local.start()

    def wblock(zrel, ys=None, e=None):
        e = core if e is None else e
        zz = (z + 8 - zrel) % 8
        return wbuf.at[zz, :, e] if ys is None else wbuf.at[zz, pl.ds(ys, 2), e]

    def wring_send(sem, zrel, ys, to):
        blk = wblock(zrel, ys)
        c = remote(blk, blk, wsend.at[sem], wrecv.at[sem], devx(x, y, to, core))
        c.start()
        sent.append(c)

    def wring_wait(sem, zrel, ys):
        blk = wblock(zrel, ys)
        remote(blk, blk, wsend.at[sem], wrecv.at[sem], devx(x, y, zp, core)).wait_recv()

    def wpair_send(zrel):
        blk = wblock(zrel)
        c = remote(blk, blk, wsend.at[12 + zrel], wrecv.at[12 + zrel], partner)
        c.start()
        sent.append(c)

    def wpair_wait(zrel):
        blk = wblock(zrel, None, other)
        remote(blk, blk, wsend.at[12 + zrel], wrecv.at[12 + zrel], partner).wait_recv()

    @pl.when(same)
    def _():
        own_local.wait()

    @pl.when(jnp.logical_not(same))
    def _():
        own_remote.wait_send()
        remote(
            wbuf.at[z, y, core], wbuf.at[z, y, core], wsend.at[0], wrecv.at[0], dev(xh, 1 - xl, y, z, other)
        ).wait_recv()

    for dy in (1, 2, 3):
        blk = wbuf.at[z, (y + 4 - dy) % 4, core]
        remote(blk, blk, wsend.at[dy], wrecv.at[dy], partner).wait_recv()

    wring_send(4, 0, None, zp)
    wring_send(8, 0, None, zm)
    wpair_send(0)
    xs.step2()
    gs.step1()
    wring_wait(4, 1, None)
    wring_send(5, 1, None, zp)
    wpair_send(1)
    wring_wait(8, 7, None)
    wring_send(9, 7, None, zm)
    wpair_send(7)
    xs.step3()
    xs.step4(0)
    wring_wait(5, 2, None)
    wring_send(6, 2, None, zp)
    wpair_send(2)
    wring_wait(9, 6, None)
    wring_send(10, 6, None, zm)
    wpair_send(6)
    xs.step4(3)
    xs.step4(1)
    gs.step2()
    wring_wait(6, 3, None)
    wring_send(7, 3, 0, zp)
    wpair_send(3)
    wring_wait(10, 5, None)
    wring_send(11, 5, 2, zm)
    wpair_send(5)
    xs.step4(2)
    gs.step3()
    xs.step5()
    wring_wait(7, 4, 0)
    wring_wait(11, 4, 2)
    wpair_send(4)
    gs.step4(0)
    for zrel in range(8):
        wpair_wait(zrel)
    x_local.wait()

    acc[...] = jnp.zeros_like(acc)

    def project_x(i, _):
        cols = pl.ds(pl.multiple_of(i * 512, 512), 512)
        lhs = xbuf[:, :, :, cols].reshape(512, 512)
        rhs = wbuf[i].reshape(512, 512)[:, :384]
        acc[:, 0:384] += jnp.dot(lhs, rhs, preferred_element_type=F32)
        return 0

    lax.fori_loop(0, 8, project_x, 0)

    for i in range(3):
        qkvg_ref[i] = acc[:, i * 128:(i + 1) * 128].astype(BF)
    gated = (qkvg_ref[1].astype(F32) * qkvg_ref[2].astype(F32)).astype(BF)
    gext[pl.ds(2, 16), core] = gated.reshape(16, 32, 128)

    own = gext.at[pl.ds(2, 16), core]
    tail = gext.at[pl.ds(16, 2), core]
    for i, (src, dst, d) in enumerate((
        (own, own, partner),
        (tail, gext.at[pl.ds(0, 2), core], devx(x, y, zp, core)),
        (tail, gext.at[pl.ds(0, 2), core], devx(x, y, zp, other)),
    )):
        c = remote(src, dst, hsend.at[1 + i], hrecv.at[1 + i], d)
        c.start()
        sent.append(c)

    gs.step4(3)
    gs.step4(1)
    gs.step4(2)
    gs.step5()
    g_local.wait()
    gall_copy = pltpu.make_async_copy(gbuf, gall_out, lsem.at[4])
    gall_copy.start()

    def project_g(i, _):
        cols = pl.ds(pl.multiple_of(i * 512, 512), 512)
        lhs = gbuf[:, :, :, cols].reshape(512, 512)
        rhs = wbuf[i].reshape(512, 512)[:, 384:512]
        acc[:, 384:512] += jnp.dot(lhs, rhs, preferred_element_type=F32)
        return 0

    lax.fori_loop(0, 8, project_g, 0)
    qkvg_ref[3] = acc[:, 384:512].astype(BF)
    gmixed = (qkvg_ref[3].astype(F32) * qkvg_ref[0].astype(F32)).astype(BF)
    mext[pl.ds(0, 16), core] = gmixed.reshape(16, 32, 128)
    mown = mext.at[pl.ds(0, 16), core]
    mhead = mext.at[pl.ds(0, 2), core]
    for i, (src, dst, d) in enumerate((
        (mown, mown, partner),
        (mhead, mext.at[pl.ds(16, 2), core], devx(x, y, zm, core)),
        (mhead, mext.at[pl.ds(16, 2), core], devx(x, y, zm, other)),
    )):
        c = remote(src, dst, hsend.at[4 + i], hrecv.at[4 + i], d)
        c.start()
        sent.append(c)

    filt_local.wait()
    filt_copy.wait_recv()
    mine = jnp.where(same, 1.0, 0.0)
    taps_out[...] = filt_own[...].astype(F32) * mine + filt_recv[...].astype(F32) * (1.0 - mine)

    def hwait(i, blk):
        remote(blk, blk, hsend.at[i], hrecv.at[i], partner).wait_recv()

    hwait(1, gext.at[pl.ds(2, 16), other])
    hwait(2, gext.at[pl.ds(0, 2), core])
    hwait(3, gext.at[pl.ds(0, 2), other])
    gext_out[128:1152] = gext[2:18].reshape(1024, 128).astype(F32)
    first = jnp.where(z == 0, 0.0, 1.0)
    gext_out[0:128] = gext[0:2].reshape(128, 128).astype(F32) * first
    hwait(4, mext.at[pl.ds(0, 16), other])
    hwait(5, mext.at[pl.ds(16, 2), core])
    hwait(6, mext.at[pl.ds(16, 2), other])
    mext_out[0:1024] = mext[0:16].reshape(1024, 128).astype(F32)
    last = jnp.where(z == 7, 0.0, 1.0)
    mext_out[1024:1152] = mext[16:18].reshape(128, 128).astype(F32) * last

    gall_copy.wait()
    xs.finish()
    gs.finish()
    for c in sent:
        c.wait_send()


def conv_kernel(qkvg, gext, mext, taps, gall, gf_ref, corr_ref, dwt_ref, corr_acc, mo):
    core = lax.axis_index("tp") % 2
    corr_acc[...] = jnp.zeros_like(corr_acc)

    def chunk(p, _):
        rows = pl.ds(pl.multiple_of(p * 32, 32), 32)
        base = pl.multiple_of((p * 2 + core) * 32, 32)
        q = qkvg[0, rows, :].astype(F32)
        gm = qkvg[3, rows, :].astype(F32)
        m = mext[pl.ds(base, 32), :]

        def taps8(jo, carry):
            mixed, back = carry
            j0 = pl.multiple_of(jo * 8, 8)
            tap = taps[pl.ds(j0, 8), :]
            for ji in range(8):
                f = tap[ji:ji + 1, :]
                g = gext[pl.ds(base + 128 - j0 - ji, 32), :]
                mixed = mixed + f * g
                prod = m * g
                corr_acc[j0 + ji] += (prod[0:8] + prod[8:16]) + (prod[16:24] + prod[24:32])
                back = back + f * mext[pl.ds(base + j0 + ji, 32), :]
            return mixed, back

        zero = jnp.zeros((32, 128), F32)
        mixed, back = lax.fori_loop(0, 16, taps8, (zero, zero))
        mo[rows, :] = (q * mixed).astype(BF)
        gf_ref[p, 0] = (gm * mixed).astype(BF)
        gf_ref[p, 1] = (back * qkvg[2, rows, :].astype(F32)).astype(BF)
        gf_ref[p, 2] = (back * qkvg[1, rows, :].astype(F32)).astype(BF)
        return 0

    lax.fori_loop(0, 16, chunk, 0)
    corr_ref[...] = jnp.sum(corr_acc[...], axis=1)

    mot = mo[...].astype(F32).T.astype(BF)

    def grad_w(i, _):
        for e in range(2):
            cols = pl.ds(pl.multiple_of(i * 512 + e * 256, 256), 256)
            dwt_ref[i, e] = jnp.dot(mot, gall[:, cols], preferred_element_type=F32).astype(BF)
        return 0

    lax.fori_loop(0, 8, grad_w, 0)


def return_kernel(
    scale,
    gf, dwt, corr,
    rgf, dw_out, fout,
    pbuf, sbuf, zbuf, tbuf, dwin, fz, fsum, fpair, ftot, fin,
    gsend, grecv, dsend, drecv, asend, arecv, osend, orecv, fsend, frecv, lsem,
):
    xh, xl, y, z, core = coords()
    x = xh * 2 + xl
    other = 1 - core
    partner = dev(xh, xl, y, z, other)
    same = xl == core
    half = y // 2

    barrier = pltpu.get_barrier_semaphore()
    pl.semaphore_signal(barrier, inc=1, device_id=partner, device_id_type=MESH)
    for r in range(1, 8):
        pl.semaphore_signal(barrier, inc=1, device_id=devx(x, y, (z + r) % 8, core), device_id_type=MESH)
    for ys in range(4):
        for cs in range(2):
            me = jnp.logical_and(same, jnp.logical_and(y == ys, core == cs))

            @pl.when(jnp.logical_not(me))
            def _():
                pl.semaphore_signal(barrier, inc=1, device_id=dev(xh, core, ys, z, cs), device_id_type=MESH)

    pl.semaphore_wait(barrier, 16 - jnp.where(same, 1, 0))

    order = (4, 3, 5, 2, 6, 1, 7, 0)
    for r in order:
        zz = (z + r) % 8
        remote(dwt.at[zz, other], pbuf.at[r], dsend.at[r], drecv.at[r], partner).start()
    for r in range(1, 8):
        zz = (z + r) % 8
        remote(corr.at[zz], fz.at[r], fsend.at[r], frecv.at[r], devx(x, y, zz, core)).start()

    def gf_copy(yp, xp):
        return remote(
            gf.at[pl.ds((yp * 2 + xp) * 2, 2)], rgf.at[y, core], gsend.at[yp * 2 + xp],
            grecv.at[y * 2 + core], dev(xh, xp, yp, z, xl),
        )

    def gf_self(yp, xp):
        return jnp.logical_and(same, jnp.logical_and(y == yp, xl == xp))

    gf_local = pltpu.make_async_copy(gf.at[pl.ds((y * 2 + xl) * 2, 2)], rgf.at[y, core], lsem.at[0])

    @pl.when(same)
    def _():
        gf_local.start()

    for yp in range(4):
        for xp in range(2):
            @pl.when(jnp.logical_not(gf_self(yp, xp)))
            def _():
                gf_copy(yp, xp).start()

    for r in order:
        zz = (z + r) % 8
        remote(pbuf.at[r], pbuf.at[r], dsend.at[r], drecv.at[r], partner).wait_recv()
        both = dwt[zz, core].astype(F32) + pbuf[r].astype(F32)
        sbuf[r] = both.astype(BF)
        if r:
            remote(sbuf.at[r], zbuf.at[r], asend.at[r], arecv.at[r], devx(x, y, zz, core)).start()

    fs = corr[z]
    for r in range(1, 8):
        remote(fz.at[r], fz.at[r], fsend.at[r], frecv.at[r], partner).wait_recv()
        fs = fs + fz[r]
    fsum[...] = fs
    fpair_copy = remote(fsum, fpair, fsend.at[0], frecv.at[0], partner)
    fpair_copy.start()
    fpair_copy.wait_recv()
    ftot[...] = (fsum[...] + fpair[...]) * scale

    fin_local = pltpu.make_async_copy(ftot, fin.at[y], lsem.at[1])

    def f_copy(yp):
        return remote(ftot, fin.at[y], fsend.at[8 + yp], frecv.at[8 + y], dev(xh, core, yp, z, xl))

    def f_self(yp):
        return jnp.logical_and(same, y == yp)

    @pl.when(same)
    def _():
        fin_local.start()

    for yp in range(4):
        @pl.when(jnp.logical_not(f_self(yp)))
        def _():
            f_copy(yp).start()

    total = sbuf[0].astype(F32)
    for r in (1, 7, 2, 6, 3, 5, 4):
        remote(zbuf.at[r], zbuf.at[r], asend.at[r], arecv.at[r], partner).wait_recv()
        total = total + zbuf[r].astype(F32)
    tbuf[...] = (total.T * scale).reshape(4, 64, 128)

    def dw_copy(k):
        yp, xp = core * 2 + k // 2, k % 2
        return remote(tbuf.at[k], dwin.at[y], osend.at[k], orecv.at[y], dev(xh, xp, yp, z, xl))

    def dw_self(k):
        yp, xp = core * 2 + k // 2, k % 2
        return jnp.logical_and(same, jnp.logical_and(y == yp, xl == xp))

    dw_here = jnp.logical_and(same, half == core)
    dw_local = pltpu.make_async_copy(tbuf.at[(y % 2) * 2 + xl], dwin.at[y], lsem.at[2])

    @pl.when(dw_here)
    def _():
        dw_local.start()

    for k in range(4):
        @pl.when(jnp.logical_not(dw_self(k)))
        def _():
            dw_copy(k).start()

    @pl.when(same)
    def _():
        fin_local.wait()

    for ys in range(4):
        @pl.when(jnp.logical_not(f_self(ys)))
        def _():
            remote(fin.at[ys], fin.at[ys], fsend.at[8 + ys], frecv.at[8 + ys], partner).wait_recv()
    for r in range(1, 8):
        remote(fin, fout.at[z], fsend.at[12 + r], frecv.at[12 + r], devx(x, y, (z + r) % 8, core)).start()
    fout_local = pltpu.make_async_copy(fin, fout.at[z], lsem.at[3])
    fout_local.start()

    @pl.when(dw_here)
    def _():
        dw_local.wait()

    for ys in range(4):
        @pl.when(jnp.logical_not(jnp.logical_and(dw_here, y == ys)))
        def _():
            remote(dwin.at[ys], dwin.at[ys], osend.at[ys], orecv.at[ys], partner).wait_recv()
        dw_out[:, ys * 128:(ys + 1) * 128] = dwin[ys]

    @pl.when(same)
    def _():
        gf_local.wait()

    for ys in range(4):
        for cs in range(2):
            me = jnp.logical_and(same, jnp.logical_and(y == ys, core == cs))

            @pl.when(jnp.logical_not(me))
            def _():
                blk = rgf.at[ys, cs]
                remote(blk, blk, gsend.at[0], grecv.at[ys * 2 + cs], partner).wait_recv()
    fout_local.wait()
    for r in range(1, 8):
        blk = fout.at[(z + 8 - r) % 8]
        remote(blk, blk, fsend.at[12 + r], frecv.at[12 + r], partner).wait_recv()

    for r in order:
        zz = (z + r) % 8
        remote(dwt.at[zz, other], pbuf.at[r], dsend.at[r], drecv.at[r], partner).wait_send()
        if r:
            remote(sbuf.at[r], zbuf.at[r], asend.at[r], arecv.at[r], partner).wait_send()
            remote(corr.at[zz], fz.at[r], fsend.at[r], frecv.at[r], partner).wait_send()
            remote(fin, fout.at[z], fsend.at[12 + r], frecv.at[12 + r], partner).wait_send()
    fpair_copy.wait_send()
    for yp in range(4):
        for xp in range(2):
            @pl.when(jnp.logical_not(gf_self(yp, xp)))
            def _():
                gf_copy(yp, xp).wait_send()

        @pl.when(jnp.logical_not(f_self(yp)))
        def _():
            f_copy(yp).wait_send()

        @pl.when(jnp.logical_not(dw_self(yp)))
        def _():
            dw_copy(yp).wait_send()


VM = pl.BlockSpec(memory_space=pltpu.VMEM)
ANY = pl.BlockSpec(memory_space=pl.ANY)
DMA = pltpu.SemaphoreType.DMA


def sds(shape, dtype):
    return jax.ShapeDtypeStruct(shape, dtype)


def on_device(block_input, featurizer, filters, out_weight, grad_output):
    f4 = featurizer.reshape(64, 3, 4, 128)
    w4 = out_weight.reshape(64, 1, 4, 128)
    fw = jnp.concatenate([f4, w4], axis=1).transpose(2, 0, 1, 3).reshape(4, 64, 512)
    filt = filters.reshape(4, 128, 128).transpose(0, 2, 1)

    qkvg, gext, mext, taps, gall = pl.pallas_call(
        gather_kernel,
        out_shape=(
            sds((4, 512, 128), BF), sds((1152, 128), F32), sds((1152, 128), F32), sds((128, 128), F32),
            sds((4, 4, 32, 4096), BF),
        ),
        in_specs=[ANY] * 4,
        out_specs=(VM, VM, VM, VM, ANY),
        scratch_shapes=[
            pltpu.VMEM((4, 4, 32, 4096), BF),
            pltpu.VMEM((4, 4, 32, 4096), BF),
            pltpu.VMEM((8, 4, 2, 64, 512), BF),
            pltpu.VMEM((512, 512), F32),
            pltpu.VMEM((18, 2, 32, 128), BF),
            pltpu.VMEM((18, 2, 32, 128), BF),
            pltpu.VMEM((128, 128), BF),
            pltpu.VMEM((128, 128), BF),
            DMA((80,)), DMA((80,)), DMA((20,)), DMA((20,)), DMA((7,)), DMA((7,)), DMA((5,)),
        ],
        compiler_params=pltpu.CompilerParams(
            collective_id=1, has_side_effects=True, vmem_limit_bytes=40 * 2**20
        ),
        name="gather_project",
    )(block_input, grad_output, fw, filt)

    gf, corr, dwt = pl.pallas_call(
        conv_kernel,
        out_shape=(sds((16, 3, 32, 128), BF), sds((128, 128), F32), sds((8, 2, 128, 256), BF)),
        in_specs=[VM] * 5,
        out_specs=(VM, VM, VM),
        scratch_shapes=[pltpu.VMEM((128, 8, 128), F32), pltpu.VMEM((512, 128), BF)],
        compiler_params=pltpu.CompilerParams(vmem_limit_bytes=40 * 2**20),
        name="filter_local",
    )(qkvg, gext, mext, taps, gall.reshape(512, 4096))

    scale = 1.0 / math.sqrt(128 * lax.axis_size("ctx"))
    rgf, dw, fout = pl.pallas_call(
        functools.partial(return_kernel, scale),
        out_shape=(sds((4, 2, 2, 3, 32, 128), BF), sds((64, 512), F32), sds((8, 4, 16, 128), F32)),
        in_specs=[VM] * 3,
        out_specs=(VM, VM, VM),
        scratch_shapes=[
            pltpu.VMEM((8, 128, 256), BF),
            pltpu.VMEM((8, 128, 256), BF),
            pltpu.VMEM((8, 128, 256), BF),
            pltpu.VMEM((4, 64, 128), F32),
            pltpu.VMEM((4, 64, 128), F32),
            pltpu.VMEM((8, 16, 128), F32),
            pltpu.VMEM((16, 128), F32),
            pltpu.VMEM((16, 128), F32),
            pltpu.VMEM((16, 128), F32),
            pltpu.VMEM((4, 16, 128), F32),
            DMA((8,)), DMA((8,)), DMA((8,)), DMA((8,)), DMA((8,)), DMA((8,)), DMA((4,)), DMA((4,)),
            DMA((20,)), DMA((20,)), DMA((4,)),
        ],
        compiler_params=pltpu.CompilerParams(
            collective_id=2, has_side_effects=True, vmem_limit_bytes=40 * 2**20
        ),
        name="sum_return",
    )(gf, dwt, corr.reshape(8, 16, 128))

    grad_features = rgf.transpose(2, 1, 4, 3, 0, 5).reshape(128, 3, 512)
    grad_filters = fout.transpose(1, 3, 0, 2).reshape(512, 128)
    return grad_features, dw, grad_filters


def solution(mesh):
    placed = (
        P(("ctx", "tp"), None),
        P("ctx", None, "tp"),
        P("tp", None),
        P("ctx", "tp"),
        P(("ctx", "tp"), None),
    )
    return jax.shard_map(
        on_device,
        mesh=mesh,
        in_specs=placed,
        out_specs=(P("ctx", None, "tp"), P("ctx", "tp"), P("tp", None)),
        check_vma=False,
    )
```

```python
import functools
import math

import jax
import jax.numpy as jnp
from jax import lax
from jax.experimental import pallas as pl
from jax.experimental.pallas import tpu as pltpu
from jax.sharding import PartitionSpec as P

MESH = pl.DeviceIdType.MESH
BF = jnp.bfloat16
F32 = jnp.float32
FP, FM, HP, HM = 0, 1, 2, 3
FAR = ((4, 3, 5, 2), (6, 1, 7, 0))


def coords():
    ctx = lax.axis_index("ctx")
    tp = lax.axis_index("tp")
    z = ctx // 8
    y = (ctx // 2) % 4
    xl = ctx % 2
    xh = tp // 2
    core = tp % 2
    return xh, xl, y, z, core


def dev(xh, xl, y, z, core):
    return ((z * 4 + y) * 2 + xl, xh * 2 + core)


def devx(x, y, z, core):
    return dev(x // 2, x % 2, y, z, core)


def slot_of(x):
    return (x % 2) * 2 + x // 2


def remote(src, dst, ssem, rsem, device):
    return pltpu.make_async_remote_copy(
        src_ref=src, dst_ref=dst, send_sem=ssem, recv_sem=rsem, device_id=device, device_id_type=MESH
    )


class Plane:
    def __init__(self, place, ssem, rsem, base, here):
        self.place, self.ssem, self.rsem, self.base = place, ssem, rsem, base
        self.x, self.y, self.z, self.core = here
        self.sent = []

    def unit(self, lr, a, b, half):
        dx, dy = (a, b) if lr == 0 else (b, a)
        return self.place((self.y + dy) % 4, slot_of((self.x + dx) % 4), lr, half)

    def neighbour(self, lr, axis, by):
        if (lr == 0) == (axis == 0):
            return devx((self.x + by) % 4, self.y, self.z, self.core)
        return devx(self.x, (self.y + by) % 4, self.z, self.core)

    def sem(self, lr, axis, a, kind):
        return self.base + lr * 20 + (kind if axis == 0 else 4 + a * 4 + kind)

    def send(self, lr, axis, a, kind):
        by = 1 if kind in (FP, HP) else 3
        back = {FP: 0, FM: 0, HP: 3, HM: 1}[kind]
        half = {FP: None, FM: None, HP: 0, HM: 1}[kind]
        place = (back, 0) if axis == 0 else (a, back)
        ref = self.unit(lr, place[0], place[1], half)
        s = self.sem(lr, axis, a, kind)
        copy = remote(ref, ref, self.ssem.at[s], self.rsem.at[s], self.neighbour(lr, axis, by))
        copy.start()
        self.sent.append(copy)

    def wait(self, lr, axis, a, kind):
        off = {FP: 3, FM: 1, HP: 2, HM: 2}[kind]
        half = {FP: None, FM: None, HP: 0, HM: 1}[kind]
        place = (off, 0) if axis == 0 else (a, off)
        dst = self.unit(lr, place[0], place[1], half)
        s = self.sem(lr, axis, a, kind)
        remote(dst, dst, self.ssem.at[s], self.rsem.at[s], self.neighbour(lr, axis, 1)).wait_recv()

    def step1(self):
        for axis in range(2):
            for lr in range(2):
                for kind in (FP, FM):
                    self.send(lr, axis, 0, kind)

    def step2(self):
        for kind, a, hkind in ((FP, 3, HP), (FM, 1, HM)):
            for lr in range(2):
                self.wait(lr, 0, 0, kind)
                self.send(lr, 0, 0, hkind)
                self.send(lr, 1, a, FP)
                self.send(lr, 1, a, FM)

    def step3(self):
        for lr in range(2):
            self.wait(lr, 0, 0, HP)
            self.wait(lr, 0, 0, HM)
            self.send(lr, 1, 2, FP)
            self.send(lr, 1, 2, FM)

    def step4(self, a):
        for kind, hkind in ((FP, HP), (FM, HM)):
            for lr in range(2):
                self.wait(lr, 1, a, kind)
                self.send(lr, 1, a, hkind)

    def step5(self):
        for a in (0, 3, 1, 2):
            for lr in range(2):
                self.wait(lr, 1, a, HP)
                self.wait(lr, 1, a, HM)

    def finish(self):
        for copy in self.sent:
            copy.wait_send()


def block_kernel(
    scale,
    x_ref, g_ref, f_ref, w_ref, filt_ref,
    gfo, dw_out, fo,
    xbuf, gbuf, wbuf, wst, fst, filt_recv, acc, qkvg, gext, mext, gx, mx, taps, corr_acc, corr, mo,
    gfb, dsend_buf, down, pbuf, sbuf, zbuf, tbuf, fz, ftot, fin, fout,
    psend, precv, wsend, wrecv, hsend, hrecv, gsend, grecv, dsend, drecv, asend, arecv, osend, orecv, fsend, frecv,
    lsem,
):
    xh, xl, y, z, core = coords()
    x = xh * 2 + xl
    here = (x, y, z, core)
    other = 1 - core
    zp, zm = (z + 1) % 8, (z + 7) % 8
    partner = dev(xh, xl, y, z, other)
    same = xl == core
    apart = jnp.logical_not(same)
    me_slot = slot_of(x)

    barrier = pltpu.get_barrier_semaphore()
    greet = [
        devx((x + 1) % 4, y, z, core), devx((x + 3) % 4, y, z, core),
        devx(x, (y + 1) % 4, z, core), devx(x, (y + 3) % 4, z, core),
        partner,
        dev(xh, 1 - xl, y, z, other),
    ] + [dev(xh, core, (y + dy) % 4, z, xl) for dy in (1, 2, 3)]
    for r in range(1, 8):
        greet += [devx(x, y, (z + r) % 8, core), devx(x, y, (z + r) % 8, other)]
    for d in greet:
        pl.semaphore_signal(barrier, inc=1, device_id=d, device_id_type=MESH)
    for ys in range(4):
        for cs in range(2):
            me = jnp.logical_and(same, jnp.logical_and(y == ys, core == cs))

            @pl.when(jnp.logical_not(me))
            def _():
                pl.semaphore_signal(barrier, inc=1, device_id=dev(xh, core, ys, z, cs), device_id_type=MESH)

    stage = [
        pltpu.make_async_copy(f_ref, wst.at[pl.ds(0, 3)], lsem.at[0]),
        pltpu.make_async_copy(w_ref, wst.at[3], lsem.at[1]),
        pltpu.make_async_copy(x_ref, xbuf.at[y, me_slot], lsem.at[2]),
        pltpu.make_async_copy(filt_ref.at[pl.ds(pl.multiple_of(y * 128, 128), 128)], fst, lsem.at[3]),
    ]
    for h in range(2):
        for k in range(4):
            zz = (z + FAR[h][k]) % 8
            stage.append(pltpu.make_async_copy(
                g_ref.at[:, pl.ds(pl.multiple_of(zz * 512, 512), 512)], gbuf.at[h, y, me_slot, k], lsem.at[4 + h * 4 + k]
            ))
    for c in stage:
        c.start()
    for c in stage:
        c.wait()
    pl.semaphore_wait(barrier, len(greet) + 8 - jnp.where(same, 1, 0))

    def place_x(yy, s, lr, half):
        cols = pl.ds(0, 4096) if half is None else pl.ds(half * 2048, 2048)
        return xbuf.at[yy, s, pl.ds(lr * 16, 16), cols]

    def place_g(h):
        def place(yy, s, lr, half):
            ks = pl.ds(0, 4) if half is None else pl.ds(half * 2, 2)
            return gbuf.at[h, yy, s, ks, pl.ds(lr * 16, 16), :]
        return place

    xs = Plane(place_x, psend, precv, 0, here)
    ga = Plane(place_g(0), psend, precv, 40, here)
    gb = Plane(place_g(1), psend, precv, 80, here)
    sent = []

    def start(c):
        c.start()
        sent.append(c)

    def wslice(yy):
        return wst.at[:, :, pl.ds(pl.multiple_of(yy * 128, 128), 128)]

    for dy in (1, 2, 3):
        yy = (y + dy) % 4
        start(remote(wslice(yy), wbuf.at[z, :, y, xl], wsend.at[dy], wrecv.at[dy], dev(xh, core, yy, z, xl)))
    own_local = pltpu.make_async_copy(wslice(y), wbuf.at[z, :, y, core], lsem.at[12])
    own_remote = remote(
        wslice(y), wbuf.at[z, :, y, xl], wsend.at[0], wrecv.at[0], dev(xh, 1 - xl, y, z, other)
    )

    @pl.when(same)
    def _():
        own_local.start()

    @pl.when(apart)
    def _():
        own_remote.start()

    filt_copy = remote(fst, filt_recv, hsend.at[0], hrecv.at[0], partner)
    start(filt_copy)
    xs.step1()

    def wblock(zrel, kinds=None, e=None):
        e = core if e is None else e
        zz = (z + 8 - zrel) % 8
        return wbuf.at[zz, :, :, e] if kinds is None else wbuf.at[zz, pl.ds(kinds, 2), :, e]

    def wring_send(sem, zrel, kinds, to):
        blk = wblock(zrel, kinds)
        start(remote(blk, blk, wsend.at[sem], wrecv.at[sem], devx(x, y, to, core)))

    def wring_wait(sem, zrel, kinds):
        blk = wblock(zrel, kinds)
        remote(blk, blk, wsend.at[sem], wrecv.at[sem], devx(x, y, zp, core)).wait_recv()

    def wpair_send(zrel):
        blk = wblock(zrel)
        start(remote(blk, blk, wsend.at[12 + zrel], wrecv.at[12 + zrel], partner))

    def wpair_wait(zrel):
        blk = wblock(zrel, None, other)
        remote(blk, blk, wsend.at[12 + zrel], wrecv.at[12 + zrel], partner).wait_recv()

    @pl.when(same)
    def _():
        own_local.wait()

    @pl.when(apart)
    def _():
        blk = wbuf.at[z, :, y, core]
        own_remote.wait_send()
        remote(blk, blk, wsend.at[0], wrecv.at[0], dev(xh, 1 - xl, y, z, other)).wait_recv()

    for dy in (1, 2, 3):
        blk = wbuf.at[z, :, (y + 4 - dy) % 4, core]
        remote(blk, blk, wsend.at[dy], wrecv.at[dy], partner).wait_recv()

    wring_send(4, 0, None, zp)
    wring_send(8, 0, None, zm)
    wpair_send(0)
    xs.step2()
    wring_wait(4, 1, None)
    wring_send(5, 1, None, zp)
    wpair_send(1)
    wring_wait(8, 7, None)
    wring_send(9, 7, None, zm)
    wpair_send(7)
    xs.step3()
    xs.step4(0)
    wring_wait(5, 2, None)
    wring_send(6, 2, None, zp)
    wpair_send(2)
    wring_wait(9, 6, None)
    wring_send(10, 6, None, zm)
    wpair_send(6)
    ga.step1()
    xs.step4(3)
    xs.step4(1)
    wring_wait(6, 3, None)
    wring_send(7, 3, 0, zp)
    wpair_send(3)
    wring_wait(10, 5, None)
    wring_send(11, 5, 2, zm)
    wpair_send(5)
    xs.step4(2)
    ga.step2()
    xs.step5()
    wring_wait(7, 4, 0)
    wring_wait(11, 4, 2)
    wpair_send(4)
    ga.step3()
    ga.step4(0)
    for zrel in range(8):
        wpair_wait(zrel)

    acc[...] = jnp.zeros_like(acc)

    def project_x(i, _):
        cols = pl.ds(pl.multiple_of(i * 512, 512), 512)
        lhs = xbuf[:, :, :, cols].reshape(512, 512)
        rhs = jnp.concatenate([wbuf[i, kind].reshape(512, 128) for kind in range(3)], axis=1)
        acc[:, 0:384] += jnp.dot(lhs, rhs, preferred_element_type=F32)
        return 0

    lax.fori_loop(0, 4, project_x, 0)
    ga.step4(3)
    gb.step1()
    lax.fori_loop(4, 8, project_x, 0)
    ga.step4(1)

    for i in range(3):
        qkvg[i] = acc[:, i * 128:(i + 1) * 128].astype(BF)
    gated = (qkvg[1].astype(F32) * qkvg[2].astype(F32)).astype(BF)
    gext[pl.ds(2, 16), core] = gated.reshape(16, 32, 128)

    own = gext.at[pl.ds(2, 16), core]
    tail = gext.at[pl.ds(16, 2), core]
    head = gext.at[pl.ds(0, 2), core]
    start(remote(own, own, hsend.at[1], hrecv.at[1], partner))
    start(remote(tail, head, hsend.at[2], hrecv.at[2], devx(x, y, zp, core)))
    start(remote(tail, head, hsend.at[3], hrecv.at[3], devx(x, y, zp, other)))
    ga.step4(2)
    gb.step2()
    ga.step5()

    def project_g(h, k):
        lhs = gbuf[h, :, :, k].reshape(512, 512)
        rhs = wbuf[(z + FAR[h][k]) % 8, 3].reshape(512, 128)
        return jnp.dot(lhs, rhs, preferred_element_type=F32)

    acc[:, 384:512] = project_g(0, 0) + project_g(0, 1)
    gb.step3()
    acc[:, 384:512] += project_g(0, 2) + project_g(0, 3)

    filt_copy.wait_recv()
    mine = jnp.where(same, 1.0, 0.0)
    taps[...] = (fst[...].astype(F32) * mine + filt_recv[...].astype(F32) * (1.0 - mine)).T

    def hwait(i, blk):
        remote(blk, blk, hsend.at[i], hrecv.at[i], partner).wait_recv()

    hwait(1, gext.at[pl.ds(2, 16), other])
    hwait(2, gext.at[pl.ds(0, 2), core])
    hwait(3, gext.at[pl.ds(0, 2), other])
    first = jnp.where(z == 0, 0.0, 1.0)
    gx[0:128] = gext[0:2].reshape(128, 128).astype(F32) * first
    gx[128:1152] = gext[2:18].reshape(1024, 128).astype(F32)
    gb.step4(0)

    zero = jnp.zeros((32, 128), F32)

    def rows_of(i):
        lo = pl.multiple_of(i * 64, 64)
        return pl.ds(lo, 32), pl.ds(lo + 32, 32), pl.multiple_of((i * 4 + core) * 32, 32)

    def mixed_pair(i, _):
        r0, r1, base = rows_of(i)

        def taps8(jo, carry):
            m0, m1 = carry
            j0 = pl.multiple_of(jo * 8, 8)
            tap = taps[pl.ds(j0, 8), :]
            for ji in range(8):
                f = tap[ji:ji + 1, :]
                m0 = m0 + f * gx[pl.ds(base + 128 - j0 - ji, 32), :]
                m1 = m1 + f * gx[pl.ds(base + 192 - j0 - ji, 32), :]
            return m0, m1

        m0, m1 = lax.fori_loop(0, 16, taps8, (zero, zero))
        acc[r0, 0:128] = m0
        acc[r1, 0:128] = m1
        return 0

    lax.fori_loop(0, 3, mixed_pair, 0)
    gb.step4(3)
    lax.fori_loop(3, 6, mixed_pair, 0)
    gb.step4(1)
    lax.fori_loop(6, 8, mixed_pair, 0)
    mo[...] = (qkvg[0].astype(F32) * acc[:, 0:128]).T.astype(BF)
    gb.step4(2)

    def grad_w(h, k):
        def term(e):
            cols = pl.ds(pl.multiple_of(e * 256, 256), 256)
            rhs = gbuf[h, :, :, k, :, cols].reshape(512, 256)
            return jnp.dot(mo[...], rhs, preferred_element_type=F32)

        i = h * 4 + k
        dsend_buf[i] = term(other).astype(BF)
        start(remote(dsend_buf.at[i], pbuf.at[i], dsend.at[i], drecv.at[i], partner))
        down[i] = term(core)

    def both_cores(h, k):
        i, r = h * 4 + k, FAR[h][k]
        remote(pbuf.at[i], pbuf.at[i], dsend.at[i], drecv.at[i], partner).wait_recv()
        down[i] = down[i] + pbuf[i].astype(F32)
        if r:
            sbuf[i] = down[i].astype(BF)
            start(remote(sbuf.at[i], zbuf.at[i], asend.at[i], arecv.at[i], devx(x, y, (z + r) % 8, core)))

    for k in range(4):
        grad_w(0, k)
    gb.step5()
    acc[:, 384:512] += project_g(1, 0) + project_g(1, 1)
    for k in range(4):
        both_cores(0, k)
    acc[:, 384:512] += project_g(1, 2) + project_g(1, 3)

    qkvg[3] = acc[:, 384:512].astype(BF)
    gmixed = (qkvg[3].astype(F32) * qkvg[0].astype(F32)).astype(BF)
    mext[pl.ds(0, 16), core] = gmixed.reshape(16, 32, 128)
    mown = mext.at[pl.ds(0, 16), core]
    mhead = mext.at[pl.ds(0, 2), core]
    mtail = mext.at[pl.ds(16, 2), core]
    start(remote(mown, mown, hsend.at[4], hrecv.at[4], partner))
    start(remote(mhead, mtail, hsend.at[5], hrecv.at[5], devx(x, y, zm, core)))
    start(remote(mhead, mtail, hsend.at[6], hrecv.at[6], devx(x, y, zm, other)))
    for k in range(4):
        grad_w(1, k)

    corr_acc[...] = jnp.zeros_like(corr_acc)

    def corr_pair(i, _):
        _, _, base = rows_of(i)
        c0 = mext[pl.ds(i * 2, 1), core].reshape(32, 128).astype(F32)
        c1 = mext[pl.ds(i * 2 + 1, 1), core].reshape(32, 128).astype(F32)

        def taps8(jo, _):
            j0 = pl.multiple_of(jo * 8, 8)
            for ji in range(8):
                p = c0 * gx[pl.ds(base + 128 - j0 - ji, 32), :] + c1 * gx[pl.ds(base + 192 - j0 - ji, 32), :]
                corr_acc[j0 + ji] += (p[0:8] + p[8:16]) + (p[16:24] + p[24:32])
            return 0

        lax.fori_loop(0, 16, taps8, 0)
        return 0

    lax.fori_loop(0, 8, corr_pair, 0)
    corr[...] = jnp.sum(corr_acc[...], axis=1).reshape(8, 2, 8, 128)
    for r in range(8):
        zz = (z + r) % 8
        for e in range(2):
            if r == 0 and e == 0:
                continue
            to = core if e == 0 else other
            s = r * 2 + e
            start(remote(corr.at[zz, to], fz.at[s], fsend.at[s], frecv.at[s], devx(x, y, zz, to)))
    for k in range(4):
        both_cores(1, k)

    hwait(4, mext.at[pl.ds(0, 16), other])
    hwait(5, mext.at[pl.ds(16, 2), core])
    hwait(6, mext.at[pl.ds(16, 2), other])
    mx[0:1024] = mext[0:16].reshape(1024, 128).astype(F32)
    last = jnp.where(z == 7, 0.0, 1.0)
    mx[1024:1152] = mext[16:18].reshape(128, 128).astype(F32) * last

    def back_pair(i, _):
        r0, r1, base = rows_of(i)

        def taps8(jo, carry):
            m0, m1 = carry
            j0 = pl.multiple_of(jo * 8, 8)
            tap = taps[pl.ds(j0, 8), :]
            for ji in range(8):
                f = tap[ji:ji + 1, :]
                m0 = m0 + f * mx[pl.ds(base + j0 + ji, 32), :]
                m1 = m1 + f * mx[pl.ds(base + 64 + j0 + ji, 32), :]
            return m0, m1

        both = lax.fori_loop(0, 16, taps8, (zero, zero))
        for n, rows in enumerate((r0, r1)):
            gfb[i, 0, n] = (qkvg[3, rows, :].astype(F32) * acc[rows, 0:128]).astype(BF)
            gfb[i, 1, n] = (both[n] * qkvg[2, rows, :].astype(F32)).astype(BF)
            gfb[i, 2, n] = (both[n] * qkvg[1, rows, :].astype(F32)).astype(BF)
        return 0

    def gf_place(ysrc, csrc):
        return gfo.at[:, :, csrc, :, pl.ds(pl.multiple_of(ysrc * 128, 128), 128)]

    def gf_copy(i):
        return remote(
            gfb.at[i], gf_place(y, core), gsend.at[i], grecv.at[y * 2 + core], dev(xh, i % 2, i // 2, z, xl)
        )

    def gf_self(i):
        return jnp.logical_and(same, jnp.logical_and(y == i // 2, xl == i % 2))

    gf_local = pltpu.make_async_copy(gfb.at[y * 2 + xl], gf_place(y, core), lsem.at[13])
    for i in range(0, 8, 2):
        lax.fori_loop(i, i + 2, back_pair, 0)
        for n in (i, i + 1):
            @pl.when(gf_self(n))
            def _():
                gf_local.start()

            @pl.when(jnp.logical_not(gf_self(n)))
            def _():
                gf_copy(n).start()

    fs = corr[z, core]
    for s in range(1, 16):
        remote(fz.at[s], fz.at[s], fsend.at[s], frecv.at[s], partner).wait_recv()
        fs = fs + fz[s]
    ftot[...] = fs * scale
    fin_local = pltpu.make_async_copy(ftot, fin.at[y, core], lsem.at[14])

    def f_copy(i):
        return remote(
            ftot, fin.at[y, core], fsend.at[16 + i], frecv.at[16 + y * 2 + core], dev(xh, i % 2, i // 2, z, xl)
        )

    @pl.when(same)
    def _():
        fin_local.start()

    for i in range(8):
        @pl.when(jnp.logical_not(gf_self(i)))
        def _():
            f_copy(i).start()

    total = down[7]
    for i in range(7):
        remote(zbuf.at[i], zbuf.at[i], asend.at[i], arecv.at[i], partner).wait_recv()
        total = total + zbuf[i].astype(F32)
    tbuf[...] = (total.T * scale).reshape(4, 64, 128)

    def dw_place(ysrc):
        return dw_out.at[:, pl.ds(pl.multiple_of(ysrc * 128, 128), 128)]

    def dw_copy(k):
        yp, xp = core * 2 + k // 2, k % 2
        return remote(tbuf.at[k], dw_place(y), osend.at[k], orecv.at[y], dev(xh, xp, yp, z, xl))

    dw_here = jnp.logical_and(same, y // 2 == core)

    def dw_self(k):
        return jnp.logical_and(dw_here, jnp.logical_and(y % 2 == k // 2, xl == k % 2))

    dw_local = pltpu.make_async_copy(tbuf.at[(y % 2) * 2 + xl], dw_place(y), lsem.at[15])

    @pl.when(dw_here)
    def _():
        dw_local.start()

    for k in range(4):
        @pl.when(jnp.logical_not(dw_self(k)))
        def _():
            dw_copy(k).start()

    @pl.when(same)
    def _():
        fin_local.wait()

    for ys in range(4):
        for cs in range(2):
            me = jnp.logical_and(same, jnp.logical_and(y == ys, core == cs))

            @pl.when(jnp.logical_not(me))
            def _():
                s = 16 + ys * 2 + cs
                blk = fin.at[ys, cs]
                remote(blk, blk, fsend.at[s], frecv.at[s], partner).wait_recv()
    for r in range(1, 8):
        start(remote(fin, fout.at[z], fsend.at[24 + r], frecv.at[24 + r], devx(x, y, (z + r) % 8, core)))
    fout[z] = fin[...]

    @pl.when(dw_here)
    def _():
        dw_local.wait()

    for ys in range(4):
        @pl.when(jnp.logical_not(jnp.logical_and(dw_here, y == ys)))
        def _():
            blk = dw_place(ys)
            remote(blk, blk, osend.at[ys], orecv.at[ys], partner).wait_recv()

    @pl.when(same)
    def _():
        gf_local.wait()

    for ys in range(4):
        for cs in range(2):
            me = jnp.logical_and(same, jnp.logical_and(y == ys, core == cs))

            @pl.when(jnp.logical_not(me))
            def _():
                blk = gf_place(ys, cs)
                remote(blk, blk, gsend.at[0], grecv.at[ys * 2 + cs], partner).wait_recv()

    for r in range(1, 8):
        blk = fout.at[(z + 8 - r) % 8]
        remote(blk, blk, fsend.at[24 + r], frecv.at[24 + r], partner).wait_recv()
    for ys in range(4):
        fo[ys * 128:(ys + 1) * 128, :] = fout[:, ys].reshape(128, 128).T

    xs.finish()
    ga.finish()
    gb.finish()
    for c in sent:
        c.wait_send()
    for i in range(8):
        @pl.when(jnp.logical_not(gf_self(i)))
        def _():
            gf_copy(i).wait_send()
            f_copy(i).wait_send()
    for k in range(4):
        @pl.when(jnp.logical_not(dw_self(k)))
        def _():
            dw_copy(k).wait_send()


VM = pl.BlockSpec(memory_space=pltpu.VMEM)
HBM = pl.BlockSpec(memory_space=pltpu.HBM)
DMA = pltpu.SemaphoreType.DMA


def sds(shape, dtype):
    return jax.ShapeDtypeStruct(shape, dtype)


def on_device(block_input, featurizer, filters, out_weight, grad_output):
    scale = 1.0 / math.sqrt(128 * lax.axis_size("ctx"))
    gf, dw, gfilt = pl.pallas_call(
        functools.partial(block_kernel, scale),
        out_shape=(sds((3, 2, 2, 32, 512), BF), sds((64, 512), F32), sds((512, 128), F32)),
        in_specs=[HBM] * 5,
        out_specs=(VM, VM, VM),
        scratch_shapes=[
            pltpu.VMEM((4, 4, 32, 4096), BF),
            pltpu.VMEM((2, 4, 4, 4, 32, 512), BF),
            pltpu.VMEM((8, 4, 4, 2, 64, 128), BF),
            pltpu.VMEM((4, 64, 512), BF),
            pltpu.VMEM((128, 128), BF),
            pltpu.VMEM((128, 128), BF),
            pltpu.VMEM((512, 512), F32),
            pltpu.VMEM((4, 512, 128), BF),
            pltpu.VMEM((18, 2, 32, 128), BF),
            pltpu.VMEM((18, 2, 32, 128), BF),
            pltpu.VMEM((1152, 128), F32),
            pltpu.VMEM((1152, 128), F32),
            pltpu.VMEM((128, 128), F32),
            pltpu.VMEM((128, 8, 128), F32),
            pltpu.VMEM((8, 2, 8, 128), F32),
            pltpu.VMEM((128, 512), BF),
            pltpu.VMEM((8, 3, 2, 32, 128), BF),
            pltpu.VMEM((8, 128, 256), BF),
            pltpu.VMEM((8, 128, 256), F32),
            pltpu.VMEM((8, 128, 256), BF),
            pltpu.VMEM((7, 128, 256), BF),
            pltpu.VMEM((7, 128, 256), BF),
            pltpu.VMEM((4, 64, 128), F32),
            pltpu.VMEM((16, 8, 128), F32),
            pltpu.VMEM((8, 128), F32),
            pltpu.VMEM((4, 2, 8, 128), F32),
            pltpu.VMEM((8, 4, 2, 8, 128), F32),
            DMA((120,)), DMA((120,)), DMA((20,)), DMA((20,)), DMA((7,)), DMA((7,)), DMA((8,)), DMA((8,)),
            DMA((8,)), DMA((8,)), DMA((7,)), DMA((7,)), DMA((4,)), DMA((4,)), DMA((32,)), DMA((32,)),
            DMA((16,)),
        ],
        compiler_params=pltpu.CompilerParams(
            collective_id=1, has_side_effects=True, vmem_limit_bytes=40 * 2**20
        ),
        name="hyena_block",
    )(block_input, grad_output, featurizer.transpose(1, 0, 2), out_weight, filters)
    return gf.reshape(3, 128, 512).transpose(1, 0, 2), dw, gfilt


def solution(mesh):
    placed = (
        P(("ctx", "tp"), None),
        P("ctx", None, "tp"),
        P("tp", None),
        P("ctx", "tp"),
        P(("ctx", "tp"), None),
    )
    return jax.shard_map(
        on_device,
        mesh=mesh,
        in_specs=placed,
        out_specs=(P("ctx", None, "tp"), P("ctx", "tp"), P("tp", None)),
        check_vma=False,
    )
```

```python
import functools
import math

import jax
import jax.numpy as jnp
from jax import lax
from jax.experimental import pallas as pl
from jax.experimental.pallas import tpu as pltpu
from jax.sharding import PartitionSpec as P

MESH = pl.DeviceIdType.MESH
BF = jnp.bfloat16
F32 = jnp.float32
FP, FM, HP, HM = 0, 1, 2, 3
FAR = ((4, 3, 5, 2), (6, 1, 7, 0))


def coords():
    ctx = lax.axis_index("ctx")
    tp = lax.axis_index("tp")
    z = ctx // 8
    y = (ctx // 2) % 4
    xl = ctx % 2
    xh = tp // 2
    core = tp % 2
    return xh, xl, y, z, core


def dev(xh, xl, y, z, core):
    return ((z * 4 + y) * 2 + xl, xh * 2 + core)


def devx(x, y, z, core):
    return dev(x // 2, x % 2, y, z, core)


def slot_of(x):
    return (x % 2) * 2 + x // 2


def remote(src, dst, ssem, rsem, device):
    return pltpu.make_async_remote_copy(
        src_ref=src, dst_ref=dst, send_sem=ssem, recv_sem=rsem, device_id=device, device_id_type=MESH
    )


class Plane:
    def __init__(self, place, ssem, rsem, base, here):
        self.place, self.ssem, self.rsem, self.base = place, ssem, rsem, base
        self.x, self.y, self.z, self.core = here
        self.sent = []

    def unit(self, lr, a, b, half):
        dx, dy = (a, b) if lr == 0 else (b, a)
        return self.place((self.y + dy) % 4, slot_of((self.x + dx) % 4), lr, half)

    def neighbour(self, lr, axis, by):
        if (lr == 0) == (axis == 0):
            return devx((self.x + by) % 4, self.y, self.z, self.core)
        return devx(self.x, (self.y + by) % 4, self.z, self.core)

    def sem(self, lr, axis, a, kind):
        return self.base + lr * 20 + (kind if axis == 0 else 4 + a * 4 + kind)

    def send(self, lr, axis, a, kind):
        by = 1 if kind in (FP, HP) else 3
        back = {FP: 0, FM: 0, HP: 3, HM: 1}[kind]
        half = {FP: None, FM: None, HP: 0, HM: 1}[kind]
        place = (back, 0) if axis == 0 else (a, back)
        ref = self.unit(lr, place[0], place[1], half)
        s = self.sem(lr, axis, a, kind)
        copy = remote(ref, ref, self.ssem.at[s], self.rsem.at[s], self.neighbour(lr, axis, by))
        copy.start()
        self.sent.append(copy)

    def wait(self, lr, axis, a, kind):
        off = {FP: 3, FM: 1, HP: 2, HM: 2}[kind]
        half = {FP: None, FM: None, HP: 0, HM: 1}[kind]
        place = (off, 0) if axis == 0 else (a, off)
        dst = self.unit(lr, place[0], place[1], half)
        s = self.sem(lr, axis, a, kind)
        remote(dst, dst, self.ssem.at[s], self.rsem.at[s], self.neighbour(lr, axis, 1)).wait_recv()

    def step1(self):
        for axis in range(2):
            for lr in range(2):
                for kind in (FP, FM):
                    self.send(lr, axis, 0, kind)

    def step2(self):
        for kind, a, hkind in ((FP, 3, HP), (FM, 1, HM)):
            for lr in range(2):
                self.wait(lr, 0, 0, kind)
                self.send(lr, 0, 0, hkind)
                self.send(lr, 1, a, FP)
                self.send(lr, 1, a, FM)

    def step3(self):
        for lr in range(2):
            self.wait(lr, 0, 0, HP)
            self.wait(lr, 0, 0, HM)
            self.send(lr, 1, 2, FP)
            self.send(lr, 1, 2, FM)

    def step4(self, a):
        for kind, hkind in ((FP, HP), (FM, HM)):
            for lr in range(2):
                self.wait(lr, 1, a, kind)
                self.send(lr, 1, a, hkind)

    def step5(self):
        for a in (0, 3, 1, 2):
            for lr in range(2):
                self.wait(lr, 1, a, HP)
                self.wait(lr, 1, a, HM)

    def finish(self):
        for copy in self.sent:
            copy.wait_send()


def block_kernel(
    scale,
    x_ref, g_ref, f_ref, w_ref, filt_ref,
    gfo, dw_out, fo,
    xbuf, gbuf, wbuf, wst, fst, filt_recv, acc, qkvg, gext, mext, gx, mx, taps, corr_acc, corr, mo,
    gfb, dsend_buf, down, pbuf, sbuf, zbuf, tbuf, fz, ftot, fin, finb, fout,
    psend, precv, wsend, wrecv, hsend, hrecv, gsend, grecv, dsend, drecv, asend, arecv, osend, orecv, fsend, frecv,
    lsem,
):
    xh, xl, y, z, core = coords()
    x = xh * 2 + xl
    here = (x, y, z, core)
    other = 1 - core
    zp, zm = (z + 1) % 8, (z + 7) % 8
    partner = dev(xh, xl, y, z, other)
    same = xl == core
    apart = jnp.logical_not(same)
    me_slot = slot_of(x)

    barrier = pltpu.get_barrier_semaphore()
    greet = [
        devx((x + 1) % 4, y, z, core), devx((x + 3) % 4, y, z, core),
        devx(x, (y + 1) % 4, z, core), devx(x, (y + 3) % 4, z, core),
        partner,
        dev(xh, 1 - xl, y, z, other),
    ] + [dev(xh, core, (y + dy) % 4, z, xl) for dy in (1, 2, 3)]
    for r in range(1, 8):
        greet += [devx(x, y, (z + r) % 8, core), devx(x, y, (z + r) % 8, other)]
    for d in greet:
        pl.semaphore_signal(barrier, inc=1, device_id=d, device_id_type=MESH)
    for ys in range(4):
        for cs in range(2):
            me = jnp.logical_and(same, jnp.logical_and(y == ys, core == cs))

            @pl.when(jnp.logical_not(me))
            def _():
                pl.semaphore_signal(barrier, inc=1, device_id=dev(xh, core, ys, z, cs), device_id_type=MESH)

    stage = [
        pltpu.make_async_copy(f_ref, wst.at[pl.ds(0, 3)], lsem.at[0]),
        pltpu.make_async_copy(w_ref, wst.at[3], lsem.at[1]),
        pltpu.make_async_copy(x_ref, xbuf.at[y, me_slot], lsem.at[2]),
        pltpu.make_async_copy(filt_ref.at[pl.ds(pl.multiple_of(y * 128, 128), 128)], fst, lsem.at[3]),
    ]
    for h in range(2):
        for k in range(4):
            zz = (z + FAR[h][k]) % 8
            stage.append(pltpu.make_async_copy(
                g_ref.at[:, pl.ds(pl.multiple_of(zz * 512, 512), 512)], gbuf.at[h, y, me_slot, k], lsem.at[4 + h * 4 + k]
            ))
    for c in stage:
        c.start()
    for c in stage:
        c.wait()
    pl.semaphore_wait(barrier, len(greet) + 8 - jnp.where(same, 1, 0))

    def place_x(yy, s, lr, half):
        cols = pl.ds(0, 4096) if half is None else pl.ds(half * 2048, 2048)
        return xbuf.at[yy, s, pl.ds(lr * 16, 16), cols]

    def place_g(h):
        def place(yy, s, lr, half):
            ks = pl.ds(0, 4) if half is None else pl.ds(half * 2, 2)
            return gbuf.at[h, yy, s, ks, pl.ds(lr * 16, 16), :]
        return place

    xs = Plane(place_x, psend, precv, 0, here)
    ga = Plane(place_g(0), psend, precv, 40, here)
    gb = Plane(place_g(1), psend, precv, 80, here)
    sent = []

    def start(c):
        c.start()
        sent.append(c)

    def wslice(yy):
        return wst.at[:, :, pl.ds(pl.multiple_of(yy * 128, 128), 128)]

    for dy in (1, 2, 3):
        yy = (y + dy) % 4
        start(remote(wslice(yy), wbuf.at[z, :, y, xl], wsend.at[dy], wrecv.at[dy], dev(xh, core, yy, z, xl)))
    own_local = pltpu.make_async_copy(wslice(y), wbuf.at[z, :, y, core], lsem.at[12])
    own_remote = remote(
        wslice(y), wbuf.at[z, :, y, xl], wsend.at[0], wrecv.at[0], dev(xh, 1 - xl, y, z, other)
    )

    @pl.when(same)
    def _():
        own_local.start()

    @pl.when(apart)
    def _():
        own_remote.start()

    xs.step1()
    filt_copy = remote(fst, filt_recv, hsend.at[0], hrecv.at[0], partner)
    start(filt_copy)

    def wblock(zrel, kinds=None, e=None):
        e = core if e is None else e
        zz = (z + 8 - zrel) % 8
        return wbuf.at[zz, :, :, e] if kinds is None else wbuf.at[zz, pl.ds(kinds, 2), :, e]

    def wring_send(sem, zrel, kinds, to):
        blk = wblock(zrel, kinds)
        start(remote(blk, blk, wsend.at[sem], wrecv.at[sem], devx(x, y, to, core)))

    def wring_wait(sem, zrel, kinds):
        blk = wblock(zrel, kinds)
        remote(blk, blk, wsend.at[sem], wrecv.at[sem], devx(x, y, zp, core)).wait_recv()

    def wpair_send(zrel):
        blk = wblock(zrel)
        start(remote(blk, blk, wsend.at[12 + zrel], wrecv.at[12 + zrel], partner))

    def wpair_wait(zrel):
        blk = wblock(zrel, None, other)
        remote(blk, blk, wsend.at[12 + zrel], wrecv.at[12 + zrel], partner).wait_recv()

    def weights_in():
        @pl.when(same)
        def _():
            own_local.wait()

        @pl.when(apart)
        def _():
            blk = wbuf.at[z, :, y, core]
            own_remote.wait_send()
            remote(blk, blk, wsend.at[0], wrecv.at[0], dev(xh, 1 - xl, y, z, other)).wait_recv()

        for dy in (1, 2, 3):
            blk = wbuf.at[z, :, (y + 4 - dy) % 4, core]
            remote(blk, blk, wsend.at[dy], wrecv.at[dy], partner).wait_recv()
        wring_send(4, 0, None, zp)
        wring_send(8, 0, None, zm)
        wpair_send(0)

    def weights_hop(n):
        last = n == 3
        wring_wait(3 + n, n, None)
        wring_send(4 + n, n, 0 if last else None, zp)
        wpair_send(n)
        wring_wait(7 + n, 8 - n, None)
        wring_send(8 + n, 8 - n, 2 if last else None, zm)
        wpair_send(8 - n)

    xs.step2()
    weights_in()
    xs.step4(0)
    xs.step3()
    ga.step1()
    weights_hop(1)
    xs.step4(3)
    xs.step4(1)
    weights_hop(2)
    ga.step2()
    xs.step4(2)
    ga.step4(0)
    weights_hop(3)
    ga.step3()
    xs.step5()
    gb.step1()
    wring_wait(7, 4, 0)
    wring_wait(11, 4, 2)
    wpair_send(4)
    for zrel in range(8):
        wpair_wait(zrel)

    acc[...] = jnp.zeros_like(acc)

    def project_x(i, _):
        cols = pl.ds(pl.multiple_of(i * 512, 512), 512)
        lhs = xbuf[:, :, :, cols].reshape(512, 512)
        rhs = jnp.concatenate([wbuf[i, kind].reshape(512, 128) for kind in range(3)], axis=1)
        acc[:, 0:384] += jnp.dot(lhs, rhs, preferred_element_type=F32)
        return 0

    lax.fori_loop(0, 4, project_x, 0)
    ga.step4(3)
    lax.fori_loop(4, 8, project_x, 0)
    ga.step4(1)

    for i in range(3):
        qkvg[i] = acc[:, i * 128:(i + 1) * 128].astype(BF)
    gated = (qkvg[1].astype(F32) * qkvg[2].astype(F32)).astype(BF)
    gext[pl.ds(2, 16), core] = gated.reshape(16, 32, 128)

    own = gext.at[pl.ds(2, 16), core]
    tail = gext.at[pl.ds(16, 2), core]
    head = gext.at[pl.ds(0, 2), core]
    start(remote(own, own, hsend.at[1], hrecv.at[1], partner))
    start(remote(tail, head, hsend.at[2], hrecv.at[2], devx(x, y, zp, core)))
    start(remote(tail, head, hsend.at[3], hrecv.at[3], devx(x, y, zp, other)))
    gb.step2()
    ga.step4(2)
    gb.step4(0)
    ga.step5()

    def project_g(h, k):
        lhs = gbuf[h, :, :, k].reshape(512, 512)
        rhs = wbuf[(z + FAR[h][k]) % 8, 3].reshape(512, 128)
        return jnp.dot(lhs, rhs, preferred_element_type=F32)

    gb.step3()
    acc[:, 384:512] = project_g(0, 0) + project_g(0, 1) + project_g(0, 2) + project_g(0, 3)

    filt_copy.wait_recv()
    mine = jnp.where(same, 1.0, 0.0)
    taps[...] = (fst[...].astype(F32) * mine + filt_recv[...].astype(F32) * (1.0 - mine)).T

    def hwait(i, blk):
        remote(blk, blk, hsend.at[i], hrecv.at[i], partner).wait_recv()

    hwait(1, gext.at[pl.ds(2, 16), other])
    hwait(2, gext.at[pl.ds(0, 2), core])
    hwait(3, gext.at[pl.ds(0, 2), other])
    first = jnp.where(z == 0, 0.0, 1.0)
    gx[0:128] = gext[0:2].reshape(128, 128).astype(F32) * first
    gx[128:1152] = gext[2:18].reshape(1024, 128).astype(F32)

    zero = jnp.zeros((32, 128), F32)

    def rows_of(i):
        lo = pl.multiple_of(i * 64, 64)
        return pl.ds(lo, 32), pl.ds(lo + 32, 32), pl.multiple_of((i * 4 + core) * 32, 32)

    def mixed_pair(i, _):
        r0, r1, base = rows_of(i)

        def taps8(jo, carry):
            m0, m1 = carry
            j0 = pl.multiple_of(jo * 8, 8)
            tap = taps[pl.ds(j0, 8), :]
            for ji in range(8):
                f = tap[ji:ji + 1, :]
                m0 = m0 + f * gx[pl.ds(base + 128 - j0 - ji, 32), :]
                m1 = m1 + f * gx[pl.ds(base + 192 - j0 - ji, 32), :]
            return m0, m1

        m0, m1 = lax.fori_loop(0, 16, taps8, (zero, zero))
        acc[r0, 0:128] = m0
        acc[r1, 0:128] = m1
        return 0

    lax.fori_loop(0, 3, mixed_pair, 0)
    gb.step4(3)
    lax.fori_loop(3, 6, mixed_pair, 0)
    gb.step4(1)
    lax.fori_loop(6, 8, mixed_pair, 0)
    mo[...] = (qkvg[0].astype(F32) * acc[:, 0:128]).T.astype(BF)

    def grad_w(h, k):
        def term(e):
            cols = pl.ds(pl.multiple_of(e * 256, 256), 256)
            rhs = gbuf[h, :, :, k, :, cols].reshape(512, 256)
            return jnp.dot(mo[...], rhs, preferred_element_type=F32)

        i = h * 4 + k
        dsend_buf[i] = term(other).astype(BF)
        start(remote(dsend_buf.at[i], pbuf.at[i], dsend.at[i], drecv.at[i], partner))
        down[i] = term(core)

    def both_cores(h, k):
        i, r = h * 4 + k, FAR[h][k]
        remote(pbuf.at[i], pbuf.at[i], dsend.at[i], drecv.at[i], partner).wait_recv()
        down[i] = down[i] + pbuf[i].astype(F32)
        if r:
            sbuf[i] = down[i].astype(BF)
            start(remote(sbuf.at[i], zbuf.at[i], asend.at[i], arecv.at[i], devx(x, y, (z + r) % 8, core)))

    for k in range(4):
        grad_w(0, k)
    gb.step4(2)
    for k in range(4):
        both_cores(0, k)
    gb.step5()
    acc[:, 384:512] += project_g(1, 0) + project_g(1, 1) + project_g(1, 2) + project_g(1, 3)

    qkvg[3] = acc[:, 384:512].astype(BF)
    gmixed = (qkvg[3].astype(F32) * qkvg[0].astype(F32)).astype(BF)
    mext[pl.ds(0, 16), core] = gmixed.reshape(16, 32, 128)
    mown = mext.at[pl.ds(0, 16), core]
    mhead = mext.at[pl.ds(0, 2), core]
    mtail = mext.at[pl.ds(16, 2), core]
    start(remote(mown, mown, hsend.at[4], hrecv.at[4], partner))
    start(remote(mhead, mtail, hsend.at[5], hrecv.at[5], devx(x, y, zm, core)))
    start(remote(mhead, mtail, hsend.at[6], hrecv.at[6], devx(x, y, zm, other)))

    corr_acc[...] = jnp.zeros_like(corr_acc)

    def corr_pair(i, _):
        _, _, base = rows_of(i)
        c0 = mext[pl.ds(i * 2, 1), core].reshape(32, 128).astype(F32)
        c1 = mext[pl.ds(i * 2 + 1, 1), core].reshape(32, 128).astype(F32)

        def taps8(jo, _):
            j0 = pl.multiple_of(jo * 8, 8)
            for ji in range(8):
                p = c0 * gx[pl.ds(base + 128 - j0 - ji, 32), :] + c1 * gx[pl.ds(base + 192 - j0 - ji, 32), :]
                corr_acc[j0 + ji] += (p[0:8] + p[8:16]) + (p[16:24] + p[24:32])
            return 0

        lax.fori_loop(0, 16, taps8, 0)
        return 0

    lax.fori_loop(0, 8, corr_pair, 0)
    corr[...] = jnp.sum(corr_acc[...], axis=1).reshape(8, 2, 8, 128)
    for r in range(8):
        zz = (z + r) % 8
        for e in range(2):
            if r == 0 and e == 0:
                continue
            to = core if e == 0 else other
            s = r * 2 + e
            start(remote(corr.at[zz, to], fz.at[s], fsend.at[s], frecv.at[s], devx(x, y, zz, to)))
    for k in range(4):
        grad_w(1, k)
    for k in range(4):
        both_cores(1, k)

    hwait(4, mext.at[pl.ds(0, 16), other])
    hwait(5, mext.at[pl.ds(16, 2), core])
    hwait(6, mext.at[pl.ds(16, 2), other])
    mx[0:1024] = mext[0:16].reshape(1024, 128).astype(F32)
    last = jnp.where(z == 7, 0.0, 1.0)
    mx[1024:1152] = mext[16:18].reshape(128, 128).astype(F32) * last

    def back_pair(i, _):
        r0, r1, base = rows_of(i)

        def taps8(jo, carry):
            m0, m1 = carry
            j0 = pl.multiple_of(jo * 8, 8)
            tap = taps[pl.ds(j0, 8), :]
            for ji in range(8):
                f = tap[ji:ji + 1, :]
                m0 = m0 + f * mx[pl.ds(base + j0 + ji, 32), :]
                m1 = m1 + f * mx[pl.ds(base + 64 + j0 + ji, 32), :]
            return m0, m1

        both = lax.fori_loop(0, 16, taps8, (zero, zero))
        for n, rows in enumerate((r0, r1)):
            gfb[i, 0, n] = (qkvg[3, rows, :].astype(F32) * acc[rows, 0:128]).astype(BF)
            gfb[i, 1, n] = (both[n] * qkvg[2, rows, :].astype(F32)).astype(BF)
            gfb[i, 2, n] = (both[n] * qkvg[1, rows, :].astype(F32)).astype(BF)
        return 0

    def gf_place(ysrc, csrc):
        return gfo.at[:, :, csrc, :, pl.ds(pl.multiple_of(ysrc * 128, 128), 128)]

    def gf_copy(i):
        return remote(
            gfb.at[i], gf_place(y, core), gsend.at[i], grecv.at[y * 2 + core], dev(xh, i % 2, i // 2, z, xl)
        )

    def gf_self(i):
        return jnp.logical_and(same, jnp.logical_and(y == i // 2, xl == i % 2))

    fin_local = pltpu.make_async_copy(ftot, fin.at[y, core], lsem.at[14])

    def f_copy(i):
        return remote(
            ftot, fin.at[y, core], fsend.at[16 + i], frecv.at[16 + y * 2 + core], dev(xh, i % 2, i // 2, z, xl)
        )

    def filters_out():
        fs = corr[z, core]
        for s in range(1, 16):
            remote(fz.at[s], fz.at[s], fsend.at[s], frecv.at[s], partner).wait_recv()
            fs = fs + fz[s]
        ftot[...] = fs * scale

        @pl.when(same)
        def _():
            fin_local.start()

        for i in range(8):
            @pl.when(jnp.logical_not(gf_self(i)))
            def _():
                f_copy(i).start()

    gf_local = pltpu.make_async_copy(gfb.at[y * 2 + xl], gf_place(y, core), lsem.at[13])
    for i in range(0, 8, 2):
        if i == 4:
            filters_out()
        lax.fori_loop(i, i + 2, back_pair, 0)
        for n in (i, i + 1):
            @pl.when(gf_self(n))
            def _():
                gf_local.start()

            @pl.when(jnp.logical_not(gf_self(n)))
            def _():
                gf_copy(n).start()

    total = down[7]
    for i in range(7):
        remote(zbuf.at[i], zbuf.at[i], asend.at[i], arecv.at[i], partner).wait_recv()
        total = total + zbuf[i].astype(F32)
    tbuf[...] = (total.T * scale).reshape(4, 64, 128)

    def dw_place(ysrc):
        return dw_out.at[:, pl.ds(pl.multiple_of(ysrc * 128, 128), 128)]

    def dw_copy(k):
        yp, xp = core * 2 + k // 2, k % 2
        return remote(tbuf.at[k], dw_place(y), osend.at[k], orecv.at[y], dev(xh, xp, yp, z, xl))

    dw_here = jnp.logical_and(same, y // 2 == core)

    def dw_self(k):
        return jnp.logical_and(dw_here, jnp.logical_and(y % 2 == k // 2, xl == k % 2))

    dw_local = pltpu.make_async_copy(tbuf.at[(y % 2) * 2 + xl], dw_place(y), lsem.at[15])

    @pl.when(dw_here)
    def _():
        dw_local.start()

    for k in range(4):
        @pl.when(jnp.logical_not(dw_self(k)))
        def _():
            dw_copy(k).start()

    @pl.when(same)
    def _():
        fin_local.wait()

    for ys in range(4):
        for cs in range(2):
            me = jnp.logical_and(same, jnp.logical_and(y == ys, core == cs))

            @pl.when(jnp.logical_not(me))
            def _():
                s = 16 + ys * 2 + cs
                blk = fin.at[ys, cs]
                remote(blk, blk, fsend.at[s], frecv.at[s], partner).wait_recv()
    finb[...] = fin[...].reshape(4, 16, 128).astype(BF)
    for r in range(1, 8):
        start(remote(finb, fout.at[z], fsend.at[24 + r], frecv.at[24 + r], devx(x, y, (z + r) % 8, core)))
    fout[z] = finb[...]

    @pl.when(dw_here)
    def _():
        dw_local.wait()

    for ys in range(4):
        @pl.when(jnp.logical_not(jnp.logical_and(dw_here, y == ys)))
        def _():
            blk = dw_place(ys)
            remote(blk, blk, osend.at[ys], orecv.at[ys], partner).wait_recv()

    @pl.when(same)
    def _():
        gf_local.wait()

    for ys in range(4):
        for cs in range(2):
            me = jnp.logical_and(same, jnp.logical_and(y == ys, core == cs))

            @pl.when(jnp.logical_not(me))
            def _():
                blk = gf_place(ys, cs)
                remote(blk, blk, gsend.at[0], grecv.at[ys * 2 + cs], partner).wait_recv()

    for r in range(1, 8):
        blk = fout.at[(z + 8 - r) % 8]
        remote(blk, blk, fsend.at[24 + r], frecv.at[24 + r], partner).wait_recv()
    for ys in range(4):
        fo[ys * 128:(ys + 1) * 128, :] = fout[:, ys].reshape(128, 128).astype(F32).T

    xs.finish()
    ga.finish()
    gb.finish()
    for c in sent:
        c.wait_send()
    for i in range(8):
        @pl.when(jnp.logical_not(gf_self(i)))
        def _():
            gf_copy(i).wait_send()
            f_copy(i).wait_send()
    for k in range(4):
        @pl.when(jnp.logical_not(dw_self(k)))
        def _():
            dw_copy(k).wait_send()


VM = pl.BlockSpec(memory_space=pltpu.VMEM)
HBM = pl.BlockSpec(memory_space=pltpu.HBM)
DMA = pltpu.SemaphoreType.DMA


def sds(shape, dtype):
    return jax.ShapeDtypeStruct(shape, dtype)


def on_device(block_input, featurizer, filters, out_weight, grad_output):
    scale = 1.0 / math.sqrt(128 * lax.axis_size("ctx"))
    gf, dw, gfilt = pl.pallas_call(
        functools.partial(block_kernel, scale),
        out_shape=(sds((3, 2, 2, 32, 512), BF), sds((64, 512), F32), sds((512, 128), F32)),
        in_specs=[HBM] * 5,
        out_specs=(VM, VM, VM),
        scratch_shapes=[
            pltpu.VMEM((4, 4, 32, 4096), BF),
            pltpu.VMEM((2, 4, 4, 4, 32, 512), BF),
            pltpu.VMEM((8, 4, 4, 2, 64, 128), BF),
            pltpu.VMEM((4, 64, 512), BF),
            pltpu.VMEM((128, 128), BF),
            pltpu.VMEM((128, 128), BF),
            pltpu.VMEM((512, 512), F32),
            pltpu.VMEM((4, 512, 128), BF),
            pltpu.VMEM((18, 2, 32, 128), BF),
            pltpu.VMEM((18, 2, 32, 128), BF),
            pltpu.VMEM((1152, 128), F32),
            pltpu.VMEM((1152, 128), F32),
            pltpu.VMEM((128, 128), F32),
            pltpu.VMEM((128, 8, 128), F32),
            pltpu.VMEM((8, 2, 8, 128), F32),
            pltpu.VMEM((128, 512), BF),
            pltpu.VMEM((8, 3, 2, 32, 128), BF),
            pltpu.VMEM((8, 128, 256), BF),
            pltpu.VMEM((8, 128, 256), F32),
            pltpu.VMEM((8, 128, 256), BF),
            pltpu.VMEM((7, 128, 256), BF),
            pltpu.VMEM((7, 128, 256), BF),
            pltpu.VMEM((4, 64, 128), F32),
            pltpu.VMEM((16, 8, 128), F32),
            pltpu.VMEM((8, 128), F32),
            pltpu.VMEM((4, 2, 8, 128), F32),
            pltpu.VMEM((4, 16, 128), BF),
            pltpu.VMEM((8, 4, 16, 128), BF),
            DMA((120,)), DMA((120,)), DMA((20,)), DMA((20,)), DMA((7,)), DMA((7,)), DMA((8,)), DMA((8,)),
            DMA((8,)), DMA((8,)), DMA((7,)), DMA((7,)), DMA((4,)), DMA((4,)), DMA((32,)), DMA((32,)),
            DMA((16,)),
        ],
        compiler_params=pltpu.CompilerParams(
            collective_id=1, has_side_effects=True, vmem_limit_bytes=60 * 2**20
        ),
        name="hyena_block",
    )(block_input, grad_output, featurizer.transpose(1, 0, 2), out_weight, filters)
    return gf.reshape(3, 128, 512).transpose(1, 0, 2), dw, gfilt


def solution(mesh):
    placed = (
        P(("ctx", "tp"), None),
        P("ctx", None, "tp"),
        P("tp", None),
        P("ctx", "tp"),
        P(("ctx", "tp"), None),
    )
    return jax.shard_map(
        on_device,
        mesh=mesh,
        in_specs=placed,
        out_specs=(P("ctx", None, "tp"), P("ctx", "tp"), P("tp", None)),
        check_vma=False,
    )
```

```python
import functools
import math

import jax
import jax.numpy as jnp
from jax import lax
from jax.experimental import pallas as pl
from jax.experimental.pallas import tpu as pltpu
from jax.sharding import PartitionSpec as P

MESH = pl.DeviceIdType.MESH
BF = jnp.bfloat16
F32 = jnp.float32
FP, FM, HP, HM = 0, 1, 2, 3
FAR = ((4, 3, 5, 2), (6, 1, 7, 0))


def coords():
    ctx = lax.axis_index("ctx")
    tp = lax.axis_index("tp")
    z = ctx // 8
    y = (ctx // 2) % 4
    xl = ctx % 2
    xh = tp // 2
    core = tp % 2
    return xh, xl, y, z, core


def dev(xh, xl, y, z, core):
    return ((z * 4 + y) * 2 + xl, xh * 2 + core)


def devx(x, y, z, core):
    return dev(x // 2, x % 2, y, z, core)


def slot_of(x):
    return (x % 2) * 2 + x // 2


def remote(src, dst, ssem, rsem, device):
    return pltpu.make_async_remote_copy(
        src_ref=src, dst_ref=dst, send_sem=ssem, recv_sem=rsem, device_id=device, device_id_type=MESH
    )


class Plane:
    def __init__(self, place, ssem, rsem, base, here):
        self.place, self.ssem, self.rsem, self.base = place, ssem, rsem, base
        self.x, self.y, self.z, self.core = here
        self.sent = []

    def unit(self, lr, a, b, half):
        dx, dy = (a, b) if lr == 0 else (b, a)
        return self.place((self.y + dy) % 4, slot_of((self.x + dx) % 4), lr, half)

    def neighbour(self, lr, axis, by):
        if (lr == 0) == (axis == 0):
            return devx((self.x + by) % 4, self.y, self.z, self.core)
        return devx(self.x, (self.y + by) % 4, self.z, self.core)

    def sem(self, lr, axis, a, kind):
        return self.base + lr * 20 + (kind if axis == 0 else 4 + a * 4 + kind)

    def send(self, lr, axis, a, kind):
        by = 1 if kind in (FP, HP) else 3
        back = {FP: 0, FM: 0, HP: 3, HM: 1}[kind]
        half = {FP: None, FM: None, HP: 0, HM: 1}[kind]
        place = (back, 0) if axis == 0 else (a, back)
        ref = self.unit(lr, place[0], place[1], half)
        s = self.sem(lr, axis, a, kind)
        copy = remote(ref, ref, self.ssem.at[s], self.rsem.at[s], self.neighbour(lr, axis, by))
        copy.start()
        self.sent.append(copy)

    def wait(self, lr, axis, a, kind):
        off = {FP: 3, FM: 1, HP: 2, HM: 2}[kind]
        half = {FP: None, FM: None, HP: 0, HM: 1}[kind]
        place = (off, 0) if axis == 0 else (a, off)
        dst = self.unit(lr, place[0], place[1], half)
        s = self.sem(lr, axis, a, kind)
        remote(dst, dst, self.ssem.at[s], self.rsem.at[s], self.neighbour(lr, axis, 1)).wait_recv()

    def step1(self):
        for axis in range(2):
            for lr in range(2):
                for kind in (FP, FM):
                    self.send(lr, axis, 0, kind)

    def step2(self):
        for kind, a, hkind in ((FP, 3, HP), (FM, 1, HM)):
            for lr in range(2):
                self.wait(lr, 0, 0, kind)
                self.send(lr, 0, 0, hkind)
                self.send(lr, 1, a, FP)
                self.send(lr, 1, a, FM)

    def step3(self):
        for lr in range(2):
            self.wait(lr, 0, 0, HP)
            self.wait(lr, 0, 0, HM)
            self.send(lr, 1, 2, FP)
            self.send(lr, 1, 2, FM)

    def step4(self, a):
        for kind, hkind in ((FP, HP), (FM, HM)):
            for lr in range(2):
                self.wait(lr, 1, a, kind)
                self.send(lr, 1, a, hkind)

    def step5(self):
        for a in (0, 3, 1, 2):
            for lr in range(2):
                self.wait(lr, 1, a, HP)
                self.wait(lr, 1, a, HM)

    def finish(self):
        for copy in self.sent:
            copy.wait_send()


def block_kernel(
    scale,
    x_ref, g_ref, f_ref, w_ref, filt_ref,
    gfo, dw_out, fo,
    xbuf, gbuf, wbuf, wst, fst, filt_recv, acc, qkvg, gext, mext, gx, mx, taps, corr_acc, corr, mo,
    gfb, dsend_buf, down, pbuf, sbuf, zbuf, tbuf, fz, ftot, fin, finb, fout,
    psend, precv, wsend, wrecv, hsend, hrecv, gsend, grecv, dsend, drecv, asend, arecv, osend, orecv, fsend, frecv,
    lsem,
):
    xh, xl, y, z, core = coords()
    x = xh * 2 + xl
    here = (x, y, z, core)
    other = 1 - core
    zp, zm = (z + 1) % 8, (z + 7) % 8
    partner = dev(xh, xl, y, z, other)
    same = xl == core
    apart = jnp.logical_not(same)
    me_slot = slot_of(x)

    barrier = pltpu.get_barrier_semaphore()
    greet = [
        devx((x + 1) % 4, y, z, core), devx((x + 3) % 4, y, z, core),
        devx(x, (y + 1) % 4, z, core), devx(x, (y + 3) % 4, z, core),
        partner,
        dev(xh, 1 - xl, y, z, other),
    ] + [dev(xh, core, (y + dy) % 4, z, xl) for dy in (1, 2, 3)]
    greet += [devx(x, y, zp, core), devx(x, y, zm, core)]
    for d in greet:
        pl.semaphore_signal(barrier, inc=1, device_id=d, device_id_type=MESH)
    stage = [
        pltpu.make_async_copy(f_ref, wst.at[pl.ds(0, 3)], lsem.at[0]),
        pltpu.make_async_copy(w_ref, wst.at[3], lsem.at[1]),
        pltpu.make_async_copy(x_ref, xbuf.at[y, me_slot], lsem.at[2]),
        pltpu.make_async_copy(filt_ref.at[pl.ds(pl.multiple_of(y * 128, 128), 128)], fst, lsem.at[3]),
    ]
    for h in range(2):
        for k in range(4):
            zz = (z + FAR[h][k]) % 8
            stage.append(pltpu.make_async_copy(
                g_ref.at[:, pl.ds(pl.multiple_of(zz * 512, 512), 512)], gbuf.at[h, y, me_slot, k], lsem.at[4 + h * 4 + k]
            ))
    for c in stage:
        c.start()
    for c in stage:
        c.wait()
    pl.semaphore_wait(barrier, len(greet))

    def place_x(yy, s, lr, half):
        cols = pl.ds(0, 4096) if half is None else pl.ds(half * 2048, 2048)
        return xbuf.at[yy, s, pl.ds(lr * 16, 16), cols]

    def place_g(h):
        def place(yy, s, lr, half):
            ks = pl.ds(0, 4) if half is None else pl.ds(half * 2, 2)
            return gbuf.at[h, yy, s, ks, pl.ds(lr * 16, 16), :]
        return place

    xs = Plane(place_x, psend, precv, 0, here)
    ga = Plane(place_g(0), psend, precv, 40, here)
    gb = Plane(place_g(1), psend, precv, 80, here)
    sent = []

    def start(c):
        c.start()
        sent.append(c)

    def wslice(yy):
        return wst.at[:, :, pl.ds(pl.multiple_of(yy * 128, 128), 128)]

    for dy in (1, 2, 3):
        yy = (y + dy) % 4
        start(remote(wslice(yy), wbuf.at[z, :, y, xl], wsend.at[dy], wrecv.at[dy], dev(xh, core, yy, z, xl)))
    own_local = pltpu.make_async_copy(wslice(y), wbuf.at[z, :, y, core], lsem.at[12])
    own_remote = remote(
        wslice(y), wbuf.at[z, :, y, xl], wsend.at[0], wrecv.at[0], dev(xh, 1 - xl, y, z, other)
    )

    @pl.when(same)
    def _():
        own_local.start()

    @pl.when(apart)
    def _():
        own_remote.start()

    xs.step1()
    filt_copy = remote(fst, filt_recv, hsend.at[0], hrecv.at[0], partner)
    start(filt_copy)

    def wblock(zrel, kinds=None, e=None):
        e = core if e is None else e
        zz = (z + 8 - zrel) % 8
        return wbuf.at[zz, :, :, e] if kinds is None else wbuf.at[zz, pl.ds(kinds, 2), :, e]

    def wring_send(plus, hop, piece):
        blk = wblock(hop - 1 if plus else (9 - hop) % 8, piece * 2)
        n = 4 + (0 if plus else 8) + (hop - 1) * 2 + piece
        start(remote(blk, blk, wsend.at[n], wrecv.at[n], devx(x, y, zp if plus else zm, core)))

    def wring_wait(plus, hop, piece):
        blk = wblock(hop if plus else 8 - hop, piece * 2)
        n = 4 + (0 if plus else 8) + (hop - 1) * 2 + piece
        remote(blk, blk, wsend.at[n], wrecv.at[n], devx(x, y, zp, core)).wait_recv()

    def wpair_send(zrel):
        blk = wblock(zrel)
        start(remote(blk, blk, wsend.at[20 + zrel], wrecv.at[20 + zrel], partner))

    def wpair_wait(zrel):
        blk = wblock(zrel, None, other)
        remote(blk, blk, wsend.at[20 + zrel], wrecv.at[20 + zrel], partner).wait_recv()

    def weights_in():
        @pl.when(same)
        def _():
            own_local.wait()

        @pl.when(apart)
        def _():
            blk = wbuf.at[z, :, y, core]
            own_remote.wait_send()
            remote(blk, blk, wsend.at[0], wrecv.at[0], dev(xh, 1 - xl, y, z, other)).wait_recv()

        for dy in (1, 2, 3):
            blk = wbuf.at[z, :, (y + 4 - dy) % 4, core]
            remote(blk, blk, wsend.at[dy], wrecv.at[dy], partner).wait_recv()
        for piece in range(2):
            wring_send(True, 1, piece)
            wring_send(False, 1, piece)
        wpair_send(0)

    def weights_hop(n):
        for piece in range(2):
            for plus in (True, False):
                if n < 4 or plus == (piece == 0):
                    wring_wait(plus, n, piece)
                    if n < 3 or (n == 3 and plus == (piece == 0)):
                        wring_send(plus, n + 1, piece)
        wpair_send(n)
        if n < 4:
            wpair_send(8 - n)

    xs.step2()
    weights_in()
    xs.step4(0)
    xs.step3()
    ga.step1()
    weights_hop(1)
    xs.step4(3)
    weights_hop(2)
    xs.step4(1)
    xs.step4(2)
    weights_hop(3)
    xs.step5()
    ga.step2()
    weights_hop(4)
    ga.step4(0)
    ga.step3()
    gb.step1()
    for zrel in range(8):
        wpair_wait(zrel)

    acc[...] = jnp.zeros_like(acc)

    def project_x(i, _):
        cols = pl.ds(pl.multiple_of(i * 512, 512), 512)
        lhs = xbuf[:, :, :, cols].reshape(512, 512)
        rhs = jnp.concatenate([wbuf[i, kind].reshape(512, 128) for kind in range(3)], axis=1)
        acc[:, 0:384] += jnp.dot(lhs, rhs, preferred_element_type=F32)
        return 0

    lax.fori_loop(0, 4, project_x, 0)
    ga.step4(3)
    lax.fori_loop(4, 8, project_x, 0)

    for i in range(3):
        qkvg[i] = acc[:, i * 128:(i + 1) * 128].astype(BF)
    gated = (qkvg[1].astype(F32) * qkvg[2].astype(F32)).astype(BF)
    gext[pl.ds(2, 16), core] = gated.reshape(16, 32, 128)

    own = gext.at[pl.ds(2, 16), core]
    tail = gext.at[pl.ds(16, 2), core]
    head = gext.at[pl.ds(0, 2), core]
    start(remote(own, own, hsend.at[1], hrecv.at[1], partner))
    start(remote(tail, head, hsend.at[2], hrecv.at[2], devx(x, y, zp, core)))
    start(remote(tail, head, hsend.at[3], hrecv.at[3], devx(x, y, zp, other)))
    ga.step4(1)
    xs.finish()
    gb.step2()
    ga.step4(2)
    gb.step4(0)

    def project_g(h, k):
        lhs = gbuf[h, :, :, k].reshape(512, 512)
        rhs = wbuf[(z + FAR[h][k]) % 8, 3].reshape(512, 128)
        return jnp.dot(lhs, rhs, preferred_element_type=F32)

    filt_copy.wait_recv()
    mine = jnp.where(same, 1.0, 0.0)
    taps[...] = (fst[...].astype(F32) * mine + filt_recv[...].astype(F32) * (1.0 - mine)).T

    def hwait(i, blk):
        remote(blk, blk, hsend.at[i], hrecv.at[i], partner).wait_recv()

    hwait(1, gext.at[pl.ds(2, 16), other])
    hwait(2, gext.at[pl.ds(0, 2), core])
    hwait(3, gext.at[pl.ds(0, 2), other])
    first = jnp.where(z == 0, 0.0, 1.0)
    gx[0:128] = gext[0:2].reshape(128, 128).astype(F32) * first
    gx[128:1152] = gext[2:18].reshape(1024, 128).astype(F32)

    zero = jnp.zeros((32, 128), F32)

    def rows_of(i):
        lo = pl.multiple_of(i * 64, 64)
        return pl.ds(lo, 32), pl.ds(lo + 32, 32), pl.multiple_of((i * 4 + core) * 32, 32)

    def mixed_pair(i, _):
        r0, r1, base = rows_of(i)

        def taps8(jo, carry):
            m0, m1 = carry
            j0 = pl.multiple_of(jo * 8, 8)
            tap = taps[pl.ds(j0, 8), :]
            for ji in range(8):
                f = tap[ji:ji + 1, :]
                m0 = m0 + f * gx[pl.ds(base + 128 - j0 - ji, 32), :]
                m1 = m1 + f * gx[pl.ds(base + 192 - j0 - ji, 32), :]
            return m0, m1

        m0, m1 = lax.fori_loop(0, 16, taps8, (zero, zero))
        acc[r0, 0:128] = m0
        acc[r1, 0:128] = m1
        return 0

    lax.fori_loop(0, 4, mixed_pair, 0)
    gb.step3()
    lax.fori_loop(4, 8, mixed_pair, 0)
    mo[...] = (qkvg[0].astype(F32) * acc[:, 0:128]).T.astype(BF)
    ga.step5()
    gb.step4(3)

    def grad_w(h, k):
        def term(e):
            cols = pl.ds(pl.multiple_of(e * 256, 256), 256)
            rhs = gbuf[h, :, :, k, :, cols].reshape(512, 256)
            return jnp.dot(mo[...], rhs, preferred_element_type=F32)

        i = h * 4 + k
        dsend_buf[i] = term(other).astype(BF)
        start(remote(dsend_buf.at[i], pbuf.at[i], dsend.at[i], drecv.at[i], partner))
        down[i] = term(core)

    def both_cores(h, k):
        i, r = h * 4 + k, FAR[h][k]
        remote(pbuf.at[i], pbuf.at[i], dsend.at[i], drecv.at[i], partner).wait_recv()
        down[i] = down[i] + pbuf[i].astype(F32)
        if r:
            sbuf[i] = down[i].astype(BF)
            start(remote(sbuf.at[i], zbuf.at[i], asend.at[i], arecv.at[i], devx(x, y, (z + r) % 8, core)))

    for k in range(4):
        grad_w(0, k)
    gb.step4(1)
    for k in range(4):
        both_cores(0, k)
    acc[:, 384:512] = project_g(0, 0) + project_g(0, 1) + project_g(0, 2) + project_g(0, 3)
    gb.step4(2)
    ga.finish()
    gb.step5()
    acc[:, 384:512] += project_g(1, 0) + project_g(1, 1) + project_g(1, 2) + project_g(1, 3)

    qkvg[3] = acc[:, 384:512].astype(BF)
    gmixed = (qkvg[3].astype(F32) * qkvg[0].astype(F32)).astype(BF)
    mext[pl.ds(0, 16), core] = gmixed.reshape(16, 32, 128)
    mown = mext.at[pl.ds(0, 16), core]
    mhead = mext.at[pl.ds(0, 2), core]
    mtail = mext.at[pl.ds(16, 2), core]
    start(remote(mown, mown, hsend.at[4], hrecv.at[4], partner))
    start(remote(mhead, mtail, hsend.at[5], hrecv.at[5], devx(x, y, zm, core)))
    start(remote(mhead, mtail, hsend.at[6], hrecv.at[6], devx(x, y, zm, other)))

    corr_acc[...] = jnp.zeros_like(corr_acc)

    def corr_pair(i, _):
        _, _, base = rows_of(i)
        c0 = mext[pl.ds(i * 2, 1), core].reshape(32, 128).astype(F32)
        c1 = mext[pl.ds(i * 2 + 1, 1), core].reshape(32, 128).astype(F32)

        def taps8(jo, _):
            j0 = pl.multiple_of(jo * 8, 8)
            for ji in range(8):
                p = c0 * gx[pl.ds(base + 128 - j0 - ji, 32), :] + c1 * gx[pl.ds(base + 192 - j0 - ji, 32), :]
                corr_acc[j0 + ji] += (p[0:8] + p[8:16]) + (p[16:24] + p[24:32])
            return 0

        lax.fori_loop(0, 16, taps8, 0)
        return 0

    lax.fori_loop(0, 8, corr_pair, 0)
    corr[...] = jnp.sum(corr_acc[...], axis=1).reshape(8, 2, 8, 128)
    for r in range(8):
        zz = (z + r) % 8
        for e in range(2):
            if r == 0 and e == 0:
                continue
            to = core if e == 0 else other
            s = r * 2 + e
            start(remote(corr.at[zz, to], fz.at[s], fsend.at[s], frecv.at[s], devx(x, y, zz, to)))
    for k in range(4):
        grad_w(1, k)
    for k in range(4):
        both_cores(1, k)

    hwait(4, mext.at[pl.ds(0, 16), other])
    hwait(5, mext.at[pl.ds(16, 2), core])
    hwait(6, mext.at[pl.ds(16, 2), other])
    mx[0:1024] = mext[0:16].reshape(1024, 128).astype(F32)
    last = jnp.where(z == 7, 0.0, 1.0)
    mx[1024:1152] = mext[16:18].reshape(128, 128).astype(F32) * last

    def back_pair(i, _):
        r0, r1, base = rows_of(i)

        def taps8(jo, carry):
            m0, m1 = carry
            j0 = pl.multiple_of(jo * 8, 8)
            tap = taps[pl.ds(j0, 8), :]
            for ji in range(8):
                f = tap[ji:ji + 1, :]
                m0 = m0 + f * mx[pl.ds(base + j0 + ji, 32), :]
                m1 = m1 + f * mx[pl.ds(base + 64 + j0 + ji, 32), :]
            return m0, m1

        both = lax.fori_loop(0, 16, taps8, (zero, zero))
        for n, rows in enumerate((r0, r1)):
            gfb[i, 0, n] = (qkvg[3, rows, :].astype(F32) * acc[rows, 0:128]).astype(BF)
            gfb[i, 1, n] = (both[n] * qkvg[2, rows, :].astype(F32)).astype(BF)
            gfb[i, 2, n] = (both[n] * qkvg[1, rows, :].astype(F32)).astype(BF)
        return 0

    def gf_place(ysrc, csrc):
        return gfo.at[:, :, csrc, :, pl.ds(pl.multiple_of(ysrc * 128, 128), 128)]

    def gf_copy(i):
        return remote(
            gfb.at[i], gf_place(y, core), gsend.at[i], grecv.at[y * 2 + core], dev(xh, i % 2, i // 2, z, xl)
        )

    def gf_self(i):
        return jnp.logical_and(same, jnp.logical_and(y == i // 2, xl == i % 2))

    fin_local = pltpu.make_async_copy(ftot, fin.at[y, core], lsem.at[14])

    def f_copy(i):
        return remote(
            ftot, fin.at[y, core], fsend.at[16 + i], frecv.at[16 + y * 2 + core], dev(xh, i % 2, i // 2, z, xl)
        )

    def filters_out():
        fs = corr[z, core]
        for s in range(1, 16):
            remote(fz.at[s], fz.at[s], fsend.at[s], frecv.at[s], partner).wait_recv()
            fs = fs + fz[s]
        ftot[...] = fs * scale

        @pl.when(same)
        def _():
            fin_local.start()

        for i in range(8):
            @pl.when(jnp.logical_not(gf_self(i)))
            def _():
                f_copy(i).start()

    gf_local = pltpu.make_async_copy(gfb.at[y * 2 + xl], gf_place(y, core), lsem.at[13])
    for i in range(0, 8, 2):
        if i == 4:
            filters_out()
        lax.fori_loop(i, i + 2, back_pair, 0)
        for n in (i, i + 1):
            @pl.when(gf_self(n))
            def _():
                gf_local.start()

            @pl.when(jnp.logical_not(gf_self(n)))
            def _():
                gf_copy(n).start()

    total = down[7]
    for i in range(7):
        remote(zbuf.at[i], zbuf.at[i], asend.at[i], arecv.at[i], partner).wait_recv()
        total = total + zbuf[i].astype(F32)
    tbuf[...] = (total.T * scale).reshape(4, 64, 128)

    def dw_place(ysrc):
        return dw_out.at[:, pl.ds(pl.multiple_of(ysrc * 128, 128), 128)]

    def dw_copy(k):
        yp, xp = core * 2 + k // 2, k % 2
        return remote(tbuf.at[k], dw_place(y), osend.at[k], orecv.at[y], dev(xh, xp, yp, z, xl))

    dw_here = jnp.logical_and(same, y // 2 == core)

    def dw_self(k):
        return jnp.logical_and(dw_here, jnp.logical_and(y % 2 == k // 2, xl == k % 2))

    dw_local = pltpu.make_async_copy(tbuf.at[(y % 2) * 2 + xl], dw_place(y), lsem.at[15])

    @pl.when(dw_here)
    def _():
        dw_local.start()

    for k in range(4):
        @pl.when(jnp.logical_not(dw_self(k)))
        def _():
            dw_copy(k).start()

    @pl.when(same)
    def _():
        fin_local.wait()

    for ys in range(4):
        for cs in range(2):
            me = jnp.logical_and(same, jnp.logical_and(y == ys, core == cs))

            @pl.when(jnp.logical_not(me))
            def _():
                s = 16 + ys * 2 + cs
                blk = fin.at[ys, cs]
                remote(blk, blk, fsend.at[s], frecv.at[s], partner).wait_recv()
    finb[...] = fin[...].reshape(4, 16, 128).astype(BF)
    for r in range(1, 8):
        start(remote(finb, fout.at[z], fsend.at[24 + r], frecv.at[24 + r], devx(x, y, (z + r) % 8, core)))
    fout[z] = finb[...]

    @pl.when(dw_here)
    def _():
        dw_local.wait()

    for ys in range(4):
        @pl.when(jnp.logical_not(jnp.logical_and(dw_here, y == ys)))
        def _():
            blk = dw_place(ys)
            remote(blk, blk, osend.at[ys], orecv.at[ys], partner).wait_recv()

    @pl.when(same)
    def _():
        gf_local.wait()

    for ys in range(4):
        for cs in range(2):
            me = jnp.logical_and(same, jnp.logical_and(y == ys, core == cs))

            @pl.when(jnp.logical_not(me))
            def _():
                blk = gf_place(ys, cs)
                remote(blk, blk, gsend.at[0], grecv.at[ys * 2 + cs], partner).wait_recv()

    gb.finish()
    for c in sent:
        c.wait_send()
    for i in range(8):
        @pl.when(jnp.logical_not(gf_self(i)))
        def _():
            gf_copy(i).wait_send()
            f_copy(i).wait_send()
    for k in range(4):
        @pl.when(jnp.logical_not(dw_self(k)))
        def _():
            dw_copy(k).wait_send()

    for r in range(1, 8):
        blk = fout.at[(z + 8 - r) % 8]
        remote(blk, blk, fsend.at[24 + r], frecv.at[24 + r], partner).wait_recv()
    for ys in range(4):
        fo[ys * 128:(ys + 1) * 128, :] = fout[:, ys].reshape(128, 128).astype(F32).T

VM = pl.BlockSpec(memory_space=pltpu.VMEM)
HBM = pl.BlockSpec(memory_space=pltpu.HBM)
DMA = pltpu.SemaphoreType.DMA


def sds(shape, dtype):
    return jax.ShapeDtypeStruct(shape, dtype)


def on_device(block_input, featurizer, filters, out_weight, grad_output):
    scale = 1.0 / math.sqrt(128 * lax.axis_size("ctx"))
    gf, dw, gfilt = pl.pallas_call(
        functools.partial(block_kernel, scale),
        out_shape=(sds((3, 2, 2, 32, 512), BF), sds((64, 512), F32), sds((512, 128), F32)),
        in_specs=[HBM] * 5,
        out_specs=(VM, VM, VM),
        scratch_shapes=[
            pltpu.VMEM((4, 4, 32, 4096), BF),
            pltpu.VMEM((2, 4, 4, 4, 32, 512), BF),
            pltpu.VMEM((8, 4, 4, 2, 64, 128), BF),
            pltpu.VMEM((4, 64, 512), BF),
            pltpu.VMEM((128, 128), BF),
            pltpu.VMEM((128, 128), BF),
            pltpu.VMEM((512, 512), F32),
            pltpu.VMEM((4, 512, 128), BF),
            pltpu.VMEM((18, 2, 32, 128), BF),
            pltpu.VMEM((18, 2, 32, 128), BF),
            pltpu.VMEM((1152, 128), F32),
            pltpu.VMEM((1152, 128), F32),
            pltpu.VMEM((128, 128), F32),
            pltpu.VMEM((128, 8, 128), F32),
            pltpu.VMEM((8, 2, 8, 128), F32),
            pltpu.VMEM((128, 512), BF),
            pltpu.VMEM((8, 3, 2, 32, 128), BF),
            pltpu.VMEM((8, 128, 256), BF),
            pltpu.VMEM((8, 128, 256), F32),
            pltpu.VMEM((8, 128, 256), BF),
            pltpu.VMEM((7, 128, 256), BF),
            pltpu.VMEM((7, 128, 256), BF),
            pltpu.VMEM((4, 64, 128), F32),
            pltpu.VMEM((16, 8, 128), F32),
            pltpu.VMEM((8, 128), F32),
            pltpu.VMEM((4, 2, 8, 128), F32),
            pltpu.VMEM((4, 16, 128), BF),
            pltpu.VMEM((8, 4, 16, 128), BF),
            DMA((120,)), DMA((120,)), DMA((28,)), DMA((28,)), DMA((7,)), DMA((7,)), DMA((8,)), DMA((8,)),
            DMA((8,)), DMA((8,)), DMA((7,)), DMA((7,)), DMA((4,)), DMA((4,)), DMA((32,)), DMA((32,)),
            DMA((16,)),
        ],
        compiler_params=pltpu.CompilerParams(
            collective_id=1, has_side_effects=True, vmem_limit_bytes=60 * 2**20
        ),
        name="hyena_block",
    )(block_input, grad_output, featurizer.transpose(1, 0, 2), out_weight, filters)
    return gf.reshape(3, 128, 512).transpose(1, 0, 2), dw, gfilt


def solution(mesh):
    placed = (
        P(("ctx", "tp"), None),
        P("ctx", None, "tp"),
        P("tp", None),
        P("ctx", "tp"),
        P(("ctx", "tp"), None),
    )
    return jax.shard_map(
        on_device,
        mesh=mesh,
        in_specs=placed,
        out_specs=(P("ctx", None, "tp"), P("ctx", "tp"), P("tp", None)),
        check_vma=False,
    )
```

```python
import functools
import math

import jax
import jax.numpy as jnp
from jax import lax
from jax.experimental import pallas as pl
from jax.experimental.pallas import tpu as pltpu
from jax.sharding import PartitionSpec as P

MESH = pl.DeviceIdType.MESH
BF = jnp.bfloat16
F32 = jnp.float32
FP, FM, HP, HM = 0, 1, 2, 3
FAR = ((4, 3, 5, 2), (6, 1, 7, 0))


def coords():
    ctx = lax.axis_index("ctx")
    tp = lax.axis_index("tp")
    z = ctx // 8
    y = (ctx // 2) % 4
    xl = ctx % 2
    xh = tp // 2
    core = tp % 2
    return xh, xl, y, z, core


def dev(xh, xl, y, z, core):
    return ((z * 4 + y) * 2 + xl, xh * 2 + core)


def devx(x, y, z, core):
    return dev(x // 2, x % 2, y, z, core)


def slot_of(x):
    return (x % 2) * 2 + x // 2


def remote(src, dst, ssem, rsem, device):
    return pltpu.make_async_remote_copy(
        src_ref=src, dst_ref=dst, send_sem=ssem, recv_sem=rsem, device_id=device, device_id_type=MESH
    )


class Plane:
    def __init__(self, place, ssem, rsem, base, here):
        self.place, self.ssem, self.rsem, self.base = place, ssem, rsem, base
        self.x, self.y, self.z, self.core = here
        self.sent = []

    def unit(self, lr, a, b, half):
        dx, dy = (a, b) if lr == 0 else (b, a)
        return self.place((self.y + dy) % 4, slot_of((self.x + dx) % 4), lr, half)

    def neighbour(self, lr, axis, by):
        if (lr == 0) == (axis == 0):
            return devx((self.x + by) % 4, self.y, self.z, self.core)
        return devx(self.x, (self.y + by) % 4, self.z, self.core)

    def sem(self, lr, axis, a, kind):
        return self.base + lr * 20 + (kind if axis == 0 else 4 + a * 4 + kind)

    def send(self, lr, axis, a, kind):
        by = 1 if kind in (FP, HP) else 3
        back = {FP: 0, FM: 0, HP: 3, HM: 1}[kind]
        half = {FP: None, FM: None, HP: 0, HM: 1}[kind]
        place = (back, 0) if axis == 0 else (a, back)
        ref = self.unit(lr, place[0], place[1], half)
        s = self.sem(lr, axis, a, kind)
        copy = remote(ref, ref, self.ssem.at[s], self.rsem.at[s], self.neighbour(lr, axis, by))
        copy.start()
        self.sent.append(copy)

    def wait(self, lr, axis, a, kind):
        off = {FP: 3, FM: 1, HP: 2, HM: 2}[kind]
        half = {FP: None, FM: None, HP: 0, HM: 1}[kind]
        place = (off, 0) if axis == 0 else (a, off)
        dst = self.unit(lr, place[0], place[1], half)
        s = self.sem(lr, axis, a, kind)
        remote(dst, dst, self.ssem.at[s], self.rsem.at[s], self.neighbour(lr, axis, 1)).wait_recv()

    def step1(self):
        for axis in range(2):
            for lr in range(2):
                for kind in (FP, FM):
                    self.send(lr, axis, 0, kind)

    def step2(self):
        for kind, a, hkind in ((FP, 3, HP), (FM, 1, HM)):
            for lr in range(2):
                self.wait(lr, 0, 0, kind)
                self.send(lr, 0, 0, hkind)
                self.send(lr, 1, a, FP)
                self.send(lr, 1, a, FM)

    def step3(self):
        for lr in range(2):
            self.wait(lr, 0, 0, HP)
            self.wait(lr, 0, 0, HM)
            self.send(lr, 1, 2, FP)
            self.send(lr, 1, 2, FM)

    def step4(self, a):
        for kind, hkind in ((FP, HP), (FM, HM)):
            for lr in range(2):
                self.wait(lr, 1, a, kind)
                self.send(lr, 1, a, hkind)

    def step5(self):
        for a in (0, 3, 1, 2):
            for lr in range(2):
                self.wait(lr, 1, a, HP)
                self.wait(lr, 1, a, HM)

    def finish(self):
        for copy in self.sent:
            copy.wait_send()


def block_kernel(
    scale,
    x_ref, g_ref, f_ref, w_ref, filt_ref,
    gfo, dw_out, fo,
    xbuf, gbuf, wbuf, wst, fst, filt_recv, acc, qkvg, gext, mext, gx, mx, taps, corr_acc, corr, mo,
    gfb, dsend_buf, down, pbuf, sbuf, zbuf, tbuf, fz, ftot, fin, finb, fout,
    psend, precv, wsend, wrecv, hsend, hrecv, gsend, grecv, dsend, drecv, asend, arecv, osend, orecv, fsend, frecv,
    lsem,
):
    xh, xl, y, z, core = coords()
    x = xh * 2 + xl
    here = (x, y, z, core)
    other = 1 - core
    zp, zm = (z + 1) % 8, (z + 7) % 8
    partner = dev(xh, xl, y, z, other)
    same = xl == core
    apart = jnp.logical_not(same)
    me_slot = slot_of(x)

    barrier = pltpu.get_barrier_semaphore()
    greet = [
        devx((x + 1) % 4, y, z, core), devx((x + 3) % 4, y, z, core),
        devx(x, (y + 1) % 4, z, core), devx(x, (y + 3) % 4, z, core),
        partner,
        dev(xh, 1 - xl, y, z, other),
    ] + [dev(xh, core, (y + dy) % 4, z, xl) for dy in (1, 2, 3)]
    greet += [devx(x, y, zp, core), devx(x, y, zm, core)]
    for d in greet:
        pl.semaphore_signal(barrier, inc=1, device_id=d, device_id_type=MESH)
    stage = [
        pltpu.make_async_copy(f_ref, wst.at[pl.ds(0, 3)], lsem.at[0]),
        pltpu.make_async_copy(w_ref, wst.at[3], lsem.at[1]),
        pltpu.make_async_copy(x_ref, xbuf.at[y, me_slot], lsem.at[2]),
        pltpu.make_async_copy(filt_ref.at[pl.ds(pl.multiple_of(y * 128, 128), 128)], fst, lsem.at[3]),
    ]
    for h in range(2):
        for k in range(4):
            zz = (z + FAR[h][k]) % 8
            stage.append(pltpu.make_async_copy(
                g_ref.at[:, pl.ds(pl.multiple_of(zz * 512, 512), 512)], gbuf.at[h, y, me_slot, k], lsem.at[4 + h * 4 + k]
            ))
    for c in stage:
        c.start()
    for c in stage:
        c.wait()
    pl.semaphore_wait(barrier, len(greet))

    def place_x(yy, s, lr, half):
        cols = pl.ds(0, 4096) if half is None else pl.ds(half * 2048, 2048)
        return xbuf.at[yy, s, pl.ds(lr * 16, 16), cols]

    def place_g(h):
        def place(yy, s, lr, half):
            ks = pl.ds(0, 4) if half is None else pl.ds(half * 2, 2)
            return gbuf.at[h, yy, s, ks, pl.ds(lr * 16, 16), :]
        return place

    xs = Plane(place_x, psend, precv, 0, here)
    ga = Plane(place_g(0), psend, precv, 40, here)
    gb = Plane(place_g(1), psend, precv, 80, here)
    sent = []

    def start(c):
        c.start()
        sent.append(c)

    def wslice(yy):
        return wst.at[:, :, pl.ds(pl.multiple_of(yy * 128, 128), 128)]

    for dy in (1, 2, 3):
        yy = (y + dy) % 4
        start(remote(wslice(yy), wbuf.at[z, :, y, xl], wsend.at[dy], wrecv.at[dy], dev(xh, core, yy, z, xl)))
    own_local = pltpu.make_async_copy(wslice(y), wbuf.at[z, :, y, core], lsem.at[12])
    own_remote = remote(
        wslice(y), wbuf.at[z, :, y, xl], wsend.at[0], wrecv.at[0], dev(xh, 1 - xl, y, z, other)
    )

    @pl.when(same)
    def _():
        own_local.start()

    @pl.when(apart)
    def _():
        own_remote.start()

    xs.step1()
    filt_copy = remote(fst, filt_recv, hsend.at[0], hrecv.at[0], partner)
    start(filt_copy)

    def wblock(zrel, kinds=None, e=None):
        e = core if e is None else e
        zz = (z + 8 - zrel) % 8
        return wbuf.at[zz, :, :, e] if kinds is None else wbuf.at[zz, pl.ds(kinds, 2), :, e]

    def wring_send(plus, hop, piece):
        blk = wblock(hop - 1 if plus else (9 - hop) % 8, piece * 2)
        n = 4 + (0 if plus else 8) + (hop - 1) * 2 + piece
        start(remote(blk, blk, wsend.at[n], wrecv.at[n], devx(x, y, zp if plus else zm, core)))

    def wring_wait(plus, hop, piece):
        blk = wblock(hop if plus else 8 - hop, piece * 2)
        n = 4 + (0 if plus else 8) + (hop - 1) * 2 + piece
        remote(blk, blk, wsend.at[n], wrecv.at[n], devx(x, y, zp, core)).wait_recv()

    def wpair_send(zrel):
        blk = wblock(zrel)
        start(remote(blk, blk, wsend.at[20 + zrel], wrecv.at[20 + zrel], partner))

    def wpair_wait(zrel):
        blk = wblock(zrel, None, other)
        remote(blk, blk, wsend.at[20 + zrel], wrecv.at[20 + zrel], partner).wait_recv()

    def weights_in():
        @pl.when(same)
        def _():
            own_local.wait()

        @pl.when(apart)
        def _():
            blk = wbuf.at[z, :, y, core]
            own_remote.wait_send()
            remote(blk, blk, wsend.at[0], wrecv.at[0], dev(xh, 1 - xl, y, z, other)).wait_recv()

        for dy in (1, 2, 3):
            blk = wbuf.at[z, :, (y + 4 - dy) % 4, core]
            remote(blk, blk, wsend.at[dy], wrecv.at[dy], partner).wait_recv()
        for piece in range(2):
            wring_send(True, 1, piece)
            wring_send(False, 1, piece)
        wpair_send(0)

    def weights_hop(n):
        for piece in range(2):
            for plus in (True, False):
                if n < 4 or plus == (piece == 0):
                    wring_wait(plus, n, piece)
                    if n < 3 or (n == 3 and plus == (piece == 0)):
                        wring_send(plus, n + 1, piece)
        wpair_send(n)
        if n < 4:
            wpair_send(8 - n)

    xs.step2()
    xs.step4(0)
    weights_in()
    xs.step3()
    ga.step1()
    xs.step4(3)
    weights_hop(1)
    xs.step4(1)
    weights_hop(2)
    xs.step4(2)
    ga.step2()
    weights_hop(3)
    ga.step4(0)
    xs.step5()
    ga.step3()
    gb.step1()
    weights_hop(4)
    for zrel in range(8):
        wpair_wait(zrel)

    acc[...] = jnp.zeros_like(acc)

    def project_x(i, _):
        cols = pl.ds(pl.multiple_of(i * 512, 512), 512)
        lhs = xbuf[:, :, :, cols].reshape(512, 512)
        rhs = jnp.concatenate([wbuf[i, kind].reshape(512, 128) for kind in range(3)], axis=1)
        acc[:, 0:384] += jnp.dot(lhs, rhs, preferred_element_type=F32)
        return 0

    lax.fori_loop(0, 4, project_x, 0)
    ga.step4(3)
    lax.fori_loop(4, 8, project_x, 0)

    for i in range(3):
        qkvg[i] = acc[:, i * 128:(i + 1) * 128].astype(BF)
    gated = (qkvg[1].astype(F32) * qkvg[2].astype(F32)).astype(BF)
    gext[pl.ds(2, 16), core] = gated.reshape(16, 32, 128)

    own = gext.at[pl.ds(2, 16), core]
    tail = gext.at[pl.ds(16, 2), core]
    head = gext.at[pl.ds(0, 2), core]
    start(remote(own, own, hsend.at[1], hrecv.at[1], partner))
    start(remote(tail, head, hsend.at[2], hrecv.at[2], devx(x, y, zp, core)))
    start(remote(tail, head, hsend.at[3], hrecv.at[3], devx(x, y, zp, other)))
    ga.step4(1)
    gb.step2()
    ga.step4(2)
    gb.step4(0)
    xs.finish()

    def project_g(h, k):
        lhs = gbuf[h, :, :, k].reshape(512, 512)
        rhs = wbuf[(z + FAR[h][k]) % 8, 3].reshape(512, 128)
        return jnp.dot(lhs, rhs, preferred_element_type=F32)

    filt_copy.wait_recv()
    mine = jnp.where(same, 1.0, 0.0)
    taps[...] = (fst[...].astype(F32) * mine + filt_recv[...].astype(F32) * (1.0 - mine)).T

    def hwait(i, blk):
        remote(blk, blk, hsend.at[i], hrecv.at[i], partner).wait_recv()

    hwait(1, gext.at[pl.ds(2, 16), other])
    hwait(2, gext.at[pl.ds(0, 2), core])
    hwait(3, gext.at[pl.ds(0, 2), other])
    first = jnp.where(z == 0, 0.0, 1.0)
    gx[0:128] = gext[0:2].reshape(128, 128).astype(F32) * first
    gx[128:1152] = gext[2:18].reshape(1024, 128).astype(F32)

    zero = jnp.zeros((32, 128), F32)

    def rows_of(i):
        lo = pl.multiple_of(i * 64, 64)
        return pl.ds(lo, 32), pl.ds(lo + 32, 32), pl.multiple_of((i * 4 + core) * 32, 32)

    def mixed_pair(i, _):
        r0, r1, base = rows_of(i)

        def taps8(jo, carry):
            m0, m1 = carry
            j0 = pl.multiple_of(jo * 8, 8)
            tap = taps[pl.ds(j0, 8), :]
            for ji in range(8):
                f = tap[ji:ji + 1, :]
                m0 = m0 + f * gx[pl.ds(base + 128 - j0 - ji, 32), :]
                m1 = m1 + f * gx[pl.ds(base + 192 - j0 - ji, 32), :]
            return m0, m1

        m0, m1 = lax.fori_loop(0, 16, taps8, (zero, zero))
        acc[r0, 0:128] = m0
        acc[r1, 0:128] = m1
        return 0

    lax.fori_loop(0, 4, mixed_pair, 0)
    gb.step3()
    lax.fori_loop(4, 8, mixed_pair, 0)
    mo[...] = (qkvg[0].astype(F32) * acc[:, 0:128]).T.astype(BF)
    ga.step5()
    gb.step4(3)

    def grad_w(h, k):
        def term(e):
            cols = pl.ds(pl.multiple_of(e * 256, 256), 256)
            rhs = gbuf[h, :, :, k, :, cols].reshape(512, 256)
            return jnp.dot(mo[...], rhs, preferred_element_type=F32)

        i = h * 4 + k
        dsend_buf[i] = term(other).astype(BF)
        start(remote(dsend_buf.at[i], pbuf.at[i], dsend.at[i], drecv.at[i], partner))
        down[i] = term(core)

    def both_cores(h, k):
        i, r = h * 4 + k, FAR[h][k]
        remote(pbuf.at[i], pbuf.at[i], dsend.at[i], drecv.at[i], partner).wait_recv()
        down[i] = down[i] + pbuf[i].astype(F32)
        if r:
            sbuf[i] = down[i].astype(BF)
            start(remote(sbuf.at[i], zbuf.at[i], asend.at[i], arecv.at[i], devx(x, y, (z + r) % 8, core)))

    for k in range(4):
        grad_w(0, k)
    gb.step4(1)
    for k in range(4):
        both_cores(0, k)
    acc[:, 384:512] = project_g(0, 0) + project_g(0, 1) + project_g(0, 2) + project_g(0, 3)
    gb.step4(2)
    ga.finish()
    gb.step5()
    acc[:, 384:512] += project_g(1, 0) + project_g(1, 1) + project_g(1, 2) + project_g(1, 3)

    qkvg[3] = acc[:, 384:512].astype(BF)
    gmixed = (qkvg[3].astype(F32) * qkvg[0].astype(F32)).astype(BF)
    mext[pl.ds(0, 16), core] = gmixed.reshape(16, 32, 128)
    mown = mext.at[pl.ds(0, 16), core]
    mhead = mext.at[pl.ds(0, 2), core]
    mtail = mext.at[pl.ds(16, 2), core]
    start(remote(mown, mown, hsend.at[4], hrecv.at[4], partner))
    start(remote(mhead, mtail, hsend.at[5], hrecv.at[5], devx(x, y, zm, core)))
    start(remote(mhead, mtail, hsend.at[6], hrecv.at[6], devx(x, y, zm, other)))

    corr_acc[...] = jnp.zeros_like(corr_acc)

    def corr_pair(i, _):
        _, _, base = rows_of(i)
        c0 = mext[pl.ds(i * 2, 1), core].reshape(32, 128).astype(F32)
        c1 = mext[pl.ds(i * 2 + 1, 1), core].reshape(32, 128).astype(F32)

        def taps8(jo, _):
            j0 = pl.multiple_of(jo * 8, 8)
            for ji in range(8):
                p = c0 * gx[pl.ds(base + 128 - j0 - ji, 32), :] + c1 * gx[pl.ds(base + 192 - j0 - ji, 32), :]
                corr_acc[j0 + ji] += (p[0:8] + p[8:16]) + (p[16:24] + p[24:32])
            return 0

        lax.fori_loop(0, 16, taps8, 0)
        return 0

    lax.fori_loop(0, 8, corr_pair, 0)
    corr[...] = jnp.sum(corr_acc[...], axis=1).reshape(8, 2, 8, 128)
    for r in range(8):
        zz = (z + r) % 8
        for e in range(2):
            if r == 0 and e == 0:
                continue
            to = core if e == 0 else other
            s = r * 2 + e
            start(remote(corr.at[zz, to], fz.at[s], fsend.at[s], frecv.at[s], devx(x, y, zz, to)))
    for k in range(4):
        grad_w(1, k)
    for k in range(4):
        both_cores(1, k)

    hwait(4, mext.at[pl.ds(0, 16), other])
    hwait(5, mext.at[pl.ds(16, 2), core])
    hwait(6, mext.at[pl.ds(16, 2), other])
    mx[0:1024] = mext[0:16].reshape(1024, 128).astype(F32)
    last = jnp.where(z == 7, 0.0, 1.0)
    mx[1024:1152] = mext[16:18].reshape(128, 128).astype(F32) * last

    def back_pair(i, _):
        r0, r1, base = rows_of(i)

        def taps8(jo, carry):
            m0, m1 = carry
            j0 = pl.multiple_of(jo * 8, 8)
            tap = taps[pl.ds(j0, 8), :]
            for ji in range(8):
                f = tap[ji:ji + 1, :]
                m0 = m0 + f * mx[pl.ds(base + j0 + ji, 32), :]
                m1 = m1 + f * mx[pl.ds(base + 64 + j0 + ji, 32), :]
            return m0, m1

        both = lax.fori_loop(0, 16, taps8, (zero, zero))
        for n, rows in enumerate((r0, r1)):
            gfb[i, 0, n] = (qkvg[3, rows, :].astype(F32) * acc[rows, 0:128]).astype(BF)
            gfb[i, 1, n] = (both[n] * qkvg[2, rows, :].astype(F32)).astype(BF)
            gfb[i, 2, n] = (both[n] * qkvg[1, rows, :].astype(F32)).astype(BF)
        return 0

    def gf_place(ysrc, csrc):
        return gfo.at[:, :, csrc, :, pl.ds(pl.multiple_of(ysrc * 128, 128), 128)]

    def gf_copy(i):
        return remote(
            gfb.at[i], gf_place(y, core), gsend.at[i], grecv.at[y * 2 + core], dev(xh, i % 2, i // 2, z, xl)
        )

    def gf_self(i):
        return jnp.logical_and(same, jnp.logical_and(y == i // 2, xl == i % 2))

    fin_local = pltpu.make_async_copy(ftot, fin.at[y, core], lsem.at[14])

    def f_copy(i):
        return remote(
            ftot, fin.at[y, core], fsend.at[16 + i], frecv.at[16 + y * 2 + core], dev(xh, i % 2, i // 2, z, xl)
        )

    def filters_out():
        fs = corr[z, core]
        for s in range(1, 16):
            remote(fz.at[s], fz.at[s], fsend.at[s], frecv.at[s], partner).wait_recv()
            fs = fs + fz[s]
        ftot[...] = fs * scale

        @pl.when(same)
        def _():
            fin_local.start()

        for i in range(8):
            @pl.when(jnp.logical_not(gf_self(i)))
            def _():
                f_copy(i).start()

    gf_local = pltpu.make_async_copy(gfb.at[y * 2 + xl], gf_place(y, core), lsem.at[13])
    for i in range(0, 8, 2):
        if i == 4:
            filters_out()
        lax.fori_loop(i, i + 2, back_pair, 0)
        for n in (i, i + 1):
            @pl.when(gf_self(n))
            def _():
                gf_local.start()

            @pl.when(jnp.logical_not(gf_self(n)))
            def _():
                gf_copy(n).start()

    total = down[7]
    for i in range(7):
        remote(zbuf.at[i], zbuf.at[i], asend.at[i], arecv.at[i], partner).wait_recv()
        total = total + zbuf[i].astype(F32)
    tbuf[...] = (total.T * scale).reshape(4, 64, 128)

    def dw_place(ysrc):
        return dw_out.at[:, pl.ds(pl.multiple_of(ysrc * 128, 128), 128)]

    def dw_copy(k):
        yp, xp = core * 2 + k // 2, k % 2
        return remote(tbuf.at[k], dw_place(y), osend.at[k], orecv.at[y], dev(xh, xp, yp, z, xl))

    dw_here = jnp.logical_and(same, y // 2 == core)

    def dw_self(k):
        return jnp.logical_and(dw_here, jnp.logical_and(y % 2 == k // 2, xl == k % 2))

    dw_local = pltpu.make_async_copy(tbuf.at[(y % 2) * 2 + xl], dw_place(y), lsem.at[15])

    @pl.when(dw_here)
    def _():
        dw_local.start()

    for k in range(4):
        @pl.when(jnp.logical_not(dw_self(k)))
        def _():
            dw_copy(k).start()

    @pl.when(same)
    def _():
        fin_local.wait()

    for ys in range(4):
        for cs in range(2):
            me = jnp.logical_and(same, jnp.logical_and(y == ys, core == cs))

            @pl.when(jnp.logical_not(me))
            def _():
                s = 16 + ys * 2 + cs
                blk = fin.at[ys, cs]
                remote(blk, blk, fsend.at[s], frecv.at[s], partner).wait_recv()
    finb[...] = fin[...].reshape(4, 16, 128).astype(BF)
    for r in range(1, 8):
        start(remote(finb, fout.at[z], fsend.at[24 + r], frecv.at[24 + r], devx(x, y, (z + r) % 8, core)))
    fout[z] = finb[...]

    @pl.when(dw_here)
    def _():
        dw_local.wait()

    for ys in range(4):
        @pl.when(jnp.logical_not(jnp.logical_and(dw_here, y == ys)))
        def _():
            blk = dw_place(ys)
            remote(blk, blk, osend.at[ys], orecv.at[ys], partner).wait_recv()

    @pl.when(same)
    def _():
        gf_local.wait()

    for ys in range(4):
        for cs in range(2):
            me = jnp.logical_and(same, jnp.logical_and(y == ys, core == cs))

            @pl.when(jnp.logical_not(me))
            def _():
                blk = gf_place(ys, cs)
                remote(blk, blk, gsend.at[0], grecv.at[ys * 2 + cs], partner).wait_recv()

    gb.finish()
    for c in sent:
        c.wait_send()
    for i in range(8):
        @pl.when(jnp.logical_not(gf_self(i)))
        def _():
            gf_copy(i).wait_send()
            f_copy(i).wait_send()
    for k in range(4):
        @pl.when(jnp.logical_not(dw_self(k)))
        def _():
            dw_copy(k).wait_send()

    for r in range(1, 8):
        blk = fout.at[(z + 8 - r) % 8]
        remote(blk, blk, fsend.at[24 + r], frecv.at[24 + r], partner).wait_recv()
    for ys in range(4):
        fo[ys * 128:(ys + 1) * 128, :] = fout[:, ys].reshape(128, 128).astype(F32).T

VM = pl.BlockSpec(memory_space=pltpu.VMEM)
HBM = pl.BlockSpec(memory_space=pltpu.HBM)
DMA = pltpu.SemaphoreType.DMA


def sds(shape, dtype):
    return jax.ShapeDtypeStruct(shape, dtype)


def on_device(block_input, featurizer, filters, out_weight, grad_output):
    scale = 1.0 / math.sqrt(128 * lax.axis_size("ctx"))
    gf, dw, gfilt = pl.pallas_call(
        functools.partial(block_kernel, scale),
        out_shape=(sds((3, 2, 2, 32, 512), BF), sds((64, 512), F32), sds((512, 128), F32)),
        in_specs=[HBM] * 5,
        out_specs=(VM, VM, VM),
        scratch_shapes=[
            pltpu.VMEM((4, 4, 32, 4096), BF),
            pltpu.VMEM((2, 4, 4, 4, 32, 512), BF),
            pltpu.VMEM((8, 4, 4, 2, 64, 128), BF),
            pltpu.VMEM((4, 64, 512), BF),
            pltpu.VMEM((128, 128), BF),
            pltpu.VMEM((128, 128), BF),
            pltpu.VMEM((512, 512), F32),
            pltpu.VMEM((4, 512, 128), BF),
            pltpu.VMEM((18, 2, 32, 128), BF),
            pltpu.VMEM((18, 2, 32, 128), BF),
            pltpu.VMEM((1152, 128), F32),
            pltpu.VMEM((1152, 128), F32),
            pltpu.VMEM((128, 128), F32),
            pltpu.VMEM((128, 8, 128), F32),
            pltpu.VMEM((8, 2, 8, 128), F32),
            pltpu.VMEM((128, 512), BF),
            pltpu.VMEM((8, 3, 2, 32, 128), BF),
            pltpu.VMEM((8, 128, 256), BF),
            pltpu.VMEM((8, 128, 256), F32),
            pltpu.VMEM((8, 128, 256), BF),
            pltpu.VMEM((7, 128, 256), BF),
            pltpu.VMEM((7, 128, 256), BF),
            pltpu.VMEM((4, 64, 128), F32),
            pltpu.VMEM((16, 8, 128), F32),
            pltpu.VMEM((8, 128), F32),
            pltpu.VMEM((4, 2, 8, 128), F32),
            pltpu.VMEM((4, 16, 128), BF),
            pltpu.VMEM((8, 4, 16, 128), BF),
            DMA((120,)), DMA((120,)), DMA((28,)), DMA((28,)), DMA((7,)), DMA((7,)), DMA((8,)), DMA((8,)),
            DMA((8,)), DMA((8,)), DMA((7,)), DMA((7,)), DMA((4,)), DMA((4,)), DMA((32,)), DMA((32,)),
            DMA((16,)),
        ],
        compiler_params=pltpu.CompilerParams(
            collective_id=1, has_side_effects=True, vmem_limit_bytes=60 * 2**20
        ),
        name="hyena_block",
    )(block_input, grad_output, featurizer.transpose(1, 0, 2), out_weight, filters)
    return gf.reshape(3, 128, 512).transpose(1, 0, 2), dw, gfilt


def solution(mesh):
    placed = (
        P(("ctx", "tp"), None),
        P("ctx", None, "tp"),
        P("tp", None),
        P("ctx", "tp"),
        P(("ctx", "tp"), None),
    )
    return jax.shard_map(
        on_device,
        mesh=mesh,
        in_specs=placed,
        out_specs=(P("ctx", None, "tp"), P("ctx", "tp"), P("tp", None)),
        check_vma=False,
    )
```

```python
import functools
import math

import jax
import jax.numpy as jnp
from jax import lax
from jax.experimental import pallas as pl
from jax.experimental.pallas import tpu as pltpu
from jax.sharding import PartitionSpec as P

MESH = pl.DeviceIdType.MESH
BF = jnp.bfloat16
F32 = jnp.float32
FP, FM, HP, HM = 0, 1, 2, 3
FAR = ((4, 3, 5, 2), (6, 1, 7, 0))


def coords():
    ctx = lax.axis_index("ctx")
    tp = lax.axis_index("tp")
    z = ctx // 8
    y = (ctx // 2) % 4
    xl = ctx % 2
    xh = tp // 2
    core = tp % 2
    return xh, xl, y, z, core


def dev(xh, xl, y, z, core):
    return ((z * 4 + y) * 2 + xl, xh * 2 + core)


def devx(x, y, z, core):
    return dev(x // 2, x % 2, y, z, core)


def slot_of(x):
    return (x % 2) * 2 + x // 2


def remote(src, dst, ssem, rsem, device):
    return pltpu.make_async_remote_copy(
        src_ref=src, dst_ref=dst, send_sem=ssem, recv_sem=rsem, device_id=device, device_id_type=MESH
    )


class Plane:
    def __init__(self, place, ssem, rsem, base, here):
        self.place, self.ssem, self.rsem, self.base = place, ssem, rsem, base
        self.x, self.y, self.z, self.core = here
        self.sent = []

    def unit(self, lr, a, b, half):
        dx, dy = (a, b) if lr == 0 else (b, a)
        return self.place((self.y + dy) % 4, slot_of((self.x + dx) % 4), lr, half)

    def neighbour(self, lr, axis, by):
        if (lr == 0) == (axis == 0):
            return devx((self.x + by) % 4, self.y, self.z, self.core)
        return devx(self.x, (self.y + by) % 4, self.z, self.core)

    def sem(self, lr, axis, a, kind):
        return self.base + lr * 20 + (kind if axis == 0 else 4 + a * 4 + kind)

    def send(self, lr, axis, a, kind):
        by = 1 if kind in (FP, HP) else 3
        back = {FP: 0, FM: 0, HP: 3, HM: 1}[kind]
        half = {FP: None, FM: None, HP: 0, HM: 1}[kind]
        place = (back, 0) if axis == 0 else (a, back)
        ref = self.unit(lr, place[0], place[1], half)
        s = self.sem(lr, axis, a, kind)
        copy = remote(ref, ref, self.ssem.at[s], self.rsem.at[s], self.neighbour(lr, axis, by))
        copy.start()
        self.sent.append(copy)

    def wait(self, lr, axis, a, kind):
        off = {FP: 3, FM: 1, HP: 2, HM: 2}[kind]
        half = {FP: None, FM: None, HP: 0, HM: 1}[kind]
        place = (off, 0) if axis == 0 else (a, off)
        dst = self.unit(lr, place[0], place[1], half)
        s = self.sem(lr, axis, a, kind)
        remote(dst, dst, self.ssem.at[s], self.rsem.at[s], self.neighbour(lr, axis, 1)).wait_recv()

    def step1(self):
        for axis in range(2):
            for lr in range(2):
                for kind in (FP, FM):
                    self.send(lr, axis, 0, kind)

    def step2(self):
        for kind, a, hkind in ((FP, 3, HP), (FM, 1, HM)):
            for lr in range(2):
                self.wait(lr, 0, 0, kind)
                self.send(lr, 0, 0, hkind)
                self.send(lr, 1, a, FP)
                self.send(lr, 1, a, FM)

    def step3(self):
        for lr in range(2):
            self.wait(lr, 0, 0, HP)
            self.wait(lr, 0, 0, HM)
            self.send(lr, 1, 2, FP)
            self.send(lr, 1, 2, FM)

    def step4(self, a):
        for kind, hkind in ((FP, HP), (FM, HM)):
            for lr in range(2):
                self.wait(lr, 1, a, kind)
                self.send(lr, 1, a, hkind)

    def step5(self):
        for a in (0, 3, 1, 2):
            for lr in range(2):
                self.wait(lr, 1, a, HP)
                self.wait(lr, 1, a, HM)

    def finish(self):
        for copy in self.sent:
            copy.wait_send()


def block_kernel(
    scale,
    x_ref, g_ref, f_ref, w_ref, filt_ref,
    gfo, dw_out, fo,
    xbuf, gbuf, wbuf, wst, fst, filt_recv, acc, qkvg, gext, mext, gx, mx, taps, corr_acc, corr, mo,
    gfb, dsend_buf, down, pbuf, sbuf, zbuf, tbuf, fz, ftot, fin, finb, fout,
    psend, precv, wsend, wrecv, hsend, hrecv, gsend, grecv, dsend, drecv, asend, arecv, osend, orecv, fsend, frecv,
    lsem,
):
    xh, xl, y, z, core = coords()
    x = xh * 2 + xl
    here = (x, y, z, core)
    other = 1 - core
    zp, zm = (z + 1) % 8, (z + 7) % 8
    partner = dev(xh, xl, y, z, other)
    same = xl == core
    apart = jnp.logical_not(same)
    me_slot = slot_of(x)

    barrier = pltpu.get_barrier_semaphore()
    greet = [
        devx((x + 1) % 4, y, z, core), devx((x + 3) % 4, y, z, core),
        devx(x, (y + 1) % 4, z, core), devx(x, (y + 3) % 4, z, core),
        partner,
        dev(xh, 1 - xl, y, z, other),
    ] + [dev(xh, core, (y + dy) % 4, z, xl) for dy in (1, 2, 3)]
    greet += [devx(x, y, zp, core), devx(x, y, zm, core)]
    for d in greet:
        pl.semaphore_signal(barrier, inc=1, device_id=d, device_id_type=MESH)
    stage = [
        pltpu.make_async_copy(f_ref, wst.at[pl.ds(0, 3)], lsem.at[0]),
        pltpu.make_async_copy(w_ref, wst.at[3], lsem.at[1]),
        pltpu.make_async_copy(x_ref, xbuf.at[y, me_slot], lsem.at[2]),
        pltpu.make_async_copy(filt_ref.at[pl.ds(pl.multiple_of(y * 128, 128), 128)], fst, lsem.at[3]),
    ]
    for h in range(2):
        for k in range(4):
            zz = (z + FAR[h][k]) % 8
            stage.append(pltpu.make_async_copy(
                g_ref.at[:, pl.ds(pl.multiple_of(zz * 512, 512), 512)], gbuf.at[h, y, me_slot, k], lsem.at[4 + h * 4 + k]
            ))
    for c in stage:
        c.start()
    for c in stage:
        c.wait()
    pl.semaphore_wait(barrier, len(greet))

    def place_x(yy, s, lr, half):
        cols = pl.ds(0, 4096) if half is None else pl.ds(half * 2048, 2048)
        return xbuf.at[yy, s, pl.ds(lr * 16, 16), cols]

    def place_g(h):
        def place(yy, s, lr, half):
            ks = pl.ds(0, 4) if half is None else pl.ds(half * 2, 2)
            return gbuf.at[h, yy, s, ks, pl.ds(lr * 16, 16), :]
        return place

    xs = Plane(place_x, psend, precv, 0, here)
    ga = Plane(place_g(0), psend, precv, 40, here)
    gb = Plane(place_g(1), psend, precv, 80, here)
    sent = []

    def start(c):
        c.start()
        sent.append(c)

    def wslice(yy):
        return wst.at[:, :, pl.ds(pl.multiple_of(yy * 128, 128), 128)]

    for dy in (1, 2, 3):
        yy = (y + dy) % 4
        start(remote(wslice(yy), wbuf.at[z, :, y, xl], wsend.at[dy], wrecv.at[dy], dev(xh, core, yy, z, xl)))
    own_local = pltpu.make_async_copy(wslice(y), wbuf.at[z, :, y, core], lsem.at[12])
    own_remote = remote(
        wslice(y), wbuf.at[z, :, y, xl], wsend.at[0], wrecv.at[0], dev(xh, 1 - xl, y, z, other)
    )

    @pl.when(same)
    def _():
        own_local.start()

    @pl.when(apart)
    def _():
        own_remote.start()

    xs.step1()
    filt_copy = remote(fst, filt_recv, hsend.at[0], hrecv.at[0], partner)
    start(filt_copy)

    def wblock(zrel, kinds=None, e=None):
        e = core if e is None else e
        zz = (z + 8 - zrel) % 8
        return wbuf.at[zz, :, :, e] if kinds is None else wbuf.at[zz, pl.ds(kinds, 2), :, e]

    def wring_send(plus, hop, piece):
        blk = wblock(hop - 1 if plus else (9 - hop) % 8, piece * 2)
        n = 4 + (0 if plus else 8) + (hop - 1) * 2 + piece
        start(remote(blk, blk, wsend.at[n], wrecv.at[n], devx(x, y, zp if plus else zm, core)))

    def wring_wait(plus, hop, piece):
        blk = wblock(hop if plus else 8 - hop, piece * 2)
        n = 4 + (0 if plus else 8) + (hop - 1) * 2 + piece
        remote(blk, blk, wsend.at[n], wrecv.at[n], devx(x, y, zp, core)).wait_recv()

    def wpair_send(zrel):
        blk = wblock(zrel)
        start(remote(blk, blk, wsend.at[20 + zrel], wrecv.at[20 + zrel], partner))

    def wpair_wait(zrel):
        blk = wblock(zrel, None, other)
        remote(blk, blk, wsend.at[20 + zrel], wrecv.at[20 + zrel], partner).wait_recv()

    def weights_in():
        @pl.when(same)
        def _():
            own_local.wait()

        @pl.when(apart)
        def _():
            blk = wbuf.at[z, :, y, core]
            own_remote.wait_send()
            remote(blk, blk, wsend.at[0], wrecv.at[0], dev(xh, 1 - xl, y, z, other)).wait_recv()

        for dy in (1, 2, 3):
            blk = wbuf.at[z, :, (y + 4 - dy) % 4, core]
            remote(blk, blk, wsend.at[dy], wrecv.at[dy], partner).wait_recv()
        for piece in range(2):
            wring_send(True, 1, piece)
            wring_send(False, 1, piece)
        wpair_send(0)

    def weights_hop(n):
        for piece in range(2):
            for plus in (True, False):
                if n < 4 or plus == (piece == 0):
                    wring_wait(plus, n, piece)
                    if n < 3 or (n == 3 and plus == (piece == 0)):
                        wring_send(plus, n + 1, piece)
        wpair_send(n)
        if n < 4:
            wpair_send(8 - n)

    xs.step2()
    xs.step4(0)
    weights_in()
    xs.step3()
    ga.step1()
    xs.step4(3)
    weights_hop(1)
    xs.step4(1)
    weights_hop(2)
    xs.step4(2)
    ga.step2()
    weights_hop(3)
    ga.step4(0)
    xs.step5()
    ga.step3()
    gb.step1()

    def project_x(zrels, fresh=False):
        total = None if fresh else acc[:, 0:384]
        for zrel in zrels:
            wpair_wait(zrel)
            i = (z + 8 - zrel) % 8
            cols = pl.ds(pl.multiple_of(i * 512, 512), 512)
            lhs = xbuf[:, :, :, cols].reshape(512, 512)
            rhs = jnp.concatenate([wbuf[i, kind].reshape(512, 128) for kind in range(3)], axis=1)
            term = jnp.dot(lhs, rhs, preferred_element_type=F32)
            total = term if total is None else total + term
        acc[:, 0:384] = total

    project_x((0, 1, 7), True)
    weights_hop(4)
    project_x((2, 6))
    ga.step4(3)
    project_x((3, 5, 4))

    for i in range(3):
        qkvg[i] = acc[:, i * 128:(i + 1) * 128].astype(BF)
    gated = (qkvg[1].astype(F32) * qkvg[2].astype(F32)).astype(BF)
    gext[pl.ds(2, 16), core] = gated.reshape(16, 32, 128)

    own = gext.at[pl.ds(2, 16), core]
    tail = gext.at[pl.ds(16, 2), core]
    head = gext.at[pl.ds(0, 2), core]
    start(remote(own, own, hsend.at[1], hrecv.at[1], partner))
    start(remote(tail, head, hsend.at[2], hrecv.at[2], devx(x, y, zp, core)))
    start(remote(tail, head, hsend.at[3], hrecv.at[3], devx(x, y, zp, other)))
    ga.step4(1)
    gb.step2()
    ga.step4(2)
    gb.step4(0)
    xs.finish()

    def project_g(h, k):
        lhs = gbuf[h, :, :, k].reshape(512, 512)
        rhs = wbuf[(z + FAR[h][k]) % 8, 3].reshape(512, 128)
        return jnp.dot(lhs, rhs, preferred_element_type=F32)

    filt_copy.wait_recv()
    mine = jnp.where(same, 1.0, 0.0)
    taps[...] = (fst[...].astype(F32) * mine + filt_recv[...].astype(F32) * (1.0 - mine)).T

    def hwait(i, blk):
        remote(blk, blk, hsend.at[i], hrecv.at[i], partner).wait_recv()

    hwait(1, gext.at[pl.ds(2, 16), other])
    hwait(2, gext.at[pl.ds(0, 2), core])
    hwait(3, gext.at[pl.ds(0, 2), other])
    first = jnp.where(z == 0, 0.0, 1.0)
    gx[0:128] = gext[0:2].reshape(128, 128).astype(F32) * first
    gx[128:1152] = gext[2:18].reshape(1024, 128).astype(F32)

    zero = jnp.zeros((32, 128), F32)

    def rows_of(i):
        lo = pl.multiple_of(i * 64, 64)
        return pl.ds(lo, 32), pl.ds(lo + 32, 32), pl.multiple_of((i * 4 + core) * 32, 32)

    def mixed_pair(i, _):
        r0, r1, base = rows_of(i)

        def taps8(jo, carry):
            m0, m1 = carry
            j0 = pl.multiple_of(jo * 8, 8)
            tap = taps[pl.ds(j0, 8), :]
            for ji in range(8):
                f = tap[ji:ji + 1, :]
                m0 = m0 + f * gx[pl.ds(base + 128 - j0 - ji, 32), :]
                m1 = m1 + f * gx[pl.ds(base + 192 - j0 - ji, 32), :]
            return m0, m1

        m0, m1 = lax.fori_loop(0, 16, taps8, (zero, zero))
        acc[r0, 0:128] = m0
        acc[r1, 0:128] = m1
        return 0

    lax.fori_loop(0, 4, mixed_pair, 0)
    gb.step3()
    lax.fori_loop(4, 8, mixed_pair, 0)
    mo[...] = (qkvg[0].astype(F32) * acc[:, 0:128]).T.astype(BF)
    ga.step5()
    gb.step4(3)

    def grad_w(h, k):
        def term(e):
            cols = pl.ds(pl.multiple_of(e * 256, 256), 256)
            rhs = gbuf[h, :, :, k, :, cols].reshape(512, 256)
            return jnp.dot(mo[...], rhs, preferred_element_type=F32)

        i = h * 4 + k
        dsend_buf[i] = term(other).astype(BF)
        start(remote(dsend_buf.at[i], pbuf.at[i], dsend.at[i], drecv.at[i], partner))
        down[i] = term(core)

    def both_cores(h, k):
        i, r = h * 4 + k, FAR[h][k]
        remote(pbuf.at[i], pbuf.at[i], dsend.at[i], drecv.at[i], partner).wait_recv()
        down[i] = down[i] + pbuf[i].astype(F32)
        if r:
            sbuf[i] = down[i].astype(BF)
            start(remote(sbuf.at[i], zbuf.at[i], asend.at[i], arecv.at[i], devx(x, y, (z + r) % 8, core)))

    for k in range(4):
        grad_w(0, k)
    gb.step4(1)
    for k in range(4):
        both_cores(0, k)
    acc[:, 384:512] = project_g(0, 0) + project_g(0, 1) + project_g(0, 2) + project_g(0, 3)
    gb.step4(2)
    ga.finish()
    gb.step5()
    acc[:, 384:512] += project_g(1, 0) + project_g(1, 1) + project_g(1, 2) + project_g(1, 3)

    qkvg[3] = acc[:, 384:512].astype(BF)
    gmixed = (qkvg[3].astype(F32) * qkvg[0].astype(F32)).astype(BF)
    mext[pl.ds(0, 16), core] = gmixed.reshape(16, 32, 128)
    mown = mext.at[pl.ds(0, 16), core]
    mhead = mext.at[pl.ds(0, 2), core]
    mtail = mext.at[pl.ds(16, 2), core]
    start(remote(mown, mown, hsend.at[4], hrecv.at[4], partner))
    start(remote(mhead, mtail, hsend.at[5], hrecv.at[5], devx(x, y, zm, core)))
    start(remote(mhead, mtail, hsend.at[6], hrecv.at[6], devx(x, y, zm, other)))

    corr_acc[...] = jnp.zeros_like(corr_acc)

    def corr_pair(i, _):
        _, _, base = rows_of(i)
        c0 = mext[pl.ds(i * 2, 1), core].reshape(32, 128).astype(F32)
        c1 = mext[pl.ds(i * 2 + 1, 1), core].reshape(32, 128).astype(F32)

        def taps8(jo, _):
            j0 = pl.multiple_of(jo * 8, 8)
            for ji in range(8):
                p = c0 * gx[pl.ds(base + 128 - j0 - ji, 32), :] + c1 * gx[pl.ds(base + 192 - j0 - ji, 32), :]
                corr_acc[j0 + ji] += (p[0:8] + p[8:16]) + (p[16:24] + p[24:32])
            return 0

        lax.fori_loop(0, 16, taps8, 0)
        return 0

    lax.fori_loop(0, 8, corr_pair, 0)
    corr[...] = jnp.sum(corr_acc[...], axis=1).reshape(8, 2, 8, 128)
    for r in range(8):
        zz = (z + r) % 8
        for e in range(2):
            if r == 0 and e == 0:
                continue
            to = core if e == 0 else other
            s = r * 2 + e
            start(remote(corr.at[zz, to], fz.at[s], fsend.at[s], frecv.at[s], devx(x, y, zz, to)))
    for k in range(4):
        grad_w(1, k)
    for k in range(4):
        both_cores(1, k)

    hwait(4, mext.at[pl.ds(0, 16), other])
    hwait(5, mext.at[pl.ds(16, 2), core])
    hwait(6, mext.at[pl.ds(16, 2), other])
    mx[0:1024] = mext[0:16].reshape(1024, 128).astype(F32)
    last = jnp.where(z == 7, 0.0, 1.0)
    mx[1024:1152] = mext[16:18].reshape(128, 128).astype(F32) * last

    def back_pair(i, _):
        r0, r1, base = rows_of(i)

        def taps8(jo, carry):
            m0, m1 = carry
            j0 = pl.multiple_of(jo * 8, 8)
            tap = taps[pl.ds(j0, 8), :]
            for ji in range(8):
                f = tap[ji:ji + 1, :]
                m0 = m0 + f * mx[pl.ds(base + j0 + ji, 32), :]
                m1 = m1 + f * mx[pl.ds(base + 64 + j0 + ji, 32), :]
            return m0, m1

        both = lax.fori_loop(0, 16, taps8, (zero, zero))
        for n, rows in enumerate((r0, r1)):
            gfb[i, 0, n] = (qkvg[3, rows, :].astype(F32) * acc[rows, 0:128]).astype(BF)
            gfb[i, 1, n] = (both[n] * qkvg[2, rows, :].astype(F32)).astype(BF)
            gfb[i, 2, n] = (both[n] * qkvg[1, rows, :].astype(F32)).astype(BF)
        return 0

    def gf_place(ysrc, csrc):
        return gfo.at[:, :, csrc, :, pl.ds(pl.multiple_of(ysrc * 128, 128), 128)]

    def gf_copy(i):
        return remote(
            gfb.at[i], gf_place(y, core), gsend.at[i], grecv.at[y * 2 + core], dev(xh, i % 2, i // 2, z, xl)
        )

    def gf_self(i):
        return jnp.logical_and(same, jnp.logical_and(y == i // 2, xl == i % 2))

    fin_local = pltpu.make_async_copy(ftot, fin.at[y, core], lsem.at[14])

    def f_copy(i):
        return remote(
            ftot, fin.at[y, core], fsend.at[16 + i], frecv.at[16 + y * 2 + core], dev(xh, i % 2, i // 2, z, xl)
        )

    def filters_out():
        fs = corr[z, core]
        for s in range(1, 16):
            remote(fz.at[s], fz.at[s], fsend.at[s], frecv.at[s], partner).wait_recv()
            fs = fs + fz[s]
        ftot[...] = fs * scale

        @pl.when(same)
        def _():
            fin_local.start()

        for i in range(8):
            @pl.when(jnp.logical_not(gf_self(i)))
            def _():
                f_copy(i).start()

    gf_local = pltpu.make_async_copy(gfb.at[y * 2 + xl], gf_place(y, core), lsem.at[13])
    for i in range(0, 8, 2):
        if i == 4:
            filters_out()
        lax.fori_loop(i, i + 2, back_pair, 0)
        for n in (i, i + 1):
            @pl.when(gf_self(n))
            def _():
                gf_local.start()

            @pl.when(jnp.logical_not(gf_self(n)))
            def _():
                gf_copy(n).start()

    total = down[7]
    for i in range(7):
        remote(zbuf.at[i], zbuf.at[i], asend.at[i], arecv.at[i], partner).wait_recv()
        total = total + zbuf[i].astype(F32)
    tbuf[...] = (total.T * scale).reshape(4, 64, 128)

    def dw_place(ysrc):
        return dw_out.at[:, pl.ds(pl.multiple_of(ysrc * 128, 128), 128)]

    def dw_copy(k):
        yp, xp = core * 2 + k // 2, k % 2
        return remote(tbuf.at[k], dw_place(y), osend.at[k], orecv.at[y], dev(xh, xp, yp, z, xl))

    dw_here = jnp.logical_and(same, y // 2 == core)

    def dw_self(k):
        return jnp.logical_and(dw_here, jnp.logical_and(y % 2 == k // 2, xl == k % 2))

    dw_local = pltpu.make_async_copy(tbuf.at[(y % 2) * 2 + xl], dw_place(y), lsem.at[15])

    @pl.when(dw_here)
    def _():
        dw_local.start()

    for k in range(4):
        @pl.when(jnp.logical_not(dw_self(k)))
        def _():
            dw_copy(k).start()

    @pl.when(same)
    def _():
        fin_local.wait()

    for ys in range(4):
        for cs in range(2):
            me = jnp.logical_and(same, jnp.logical_and(y == ys, core == cs))

            @pl.when(jnp.logical_not(me))
            def _():
                s = 16 + ys * 2 + cs
                blk = fin.at[ys, cs]
                remote(blk, blk, fsend.at[s], frecv.at[s], partner).wait_recv()
    finb[...] = fin[...].reshape(4, 16, 128).astype(BF)
    for r in range(1, 8):
        start(remote(finb, fout.at[z], fsend.at[24 + r], frecv.at[24 + r], devx(x, y, (z + r) % 8, core)))
    fout[z] = finb[...]

    @pl.when(dw_here)
    def _():
        dw_local.wait()

    for ys in range(4):
        @pl.when(jnp.logical_not(jnp.logical_and(dw_here, y == ys)))
        def _():
            blk = dw_place(ys)
            remote(blk, blk, osend.at[ys], orecv.at[ys], partner).wait_recv()

    @pl.when(same)
    def _():
        gf_local.wait()

    for ys in range(4):
        for cs in range(2):
            me = jnp.logical_and(same, jnp.logical_and(y == ys, core == cs))

            @pl.when(jnp.logical_not(me))
            def _():
                blk = gf_place(ys, cs)
                remote(blk, blk, gsend.at[0], grecv.at[ys * 2 + cs], partner).wait_recv()

    gb.finish()
    for c in sent:
        c.wait_send()
    for i in range(8):
        @pl.when(jnp.logical_not(gf_self(i)))
        def _():
            gf_copy(i).wait_send()
            f_copy(i).wait_send()
    for k in range(4):
        @pl.when(jnp.logical_not(dw_self(k)))
        def _():
            dw_copy(k).wait_send()

    for r in range(1, 8):
        blk = fout.at[(z + 8 - r) % 8]
        remote(blk, blk, fsend.at[24 + r], frecv.at[24 + r], partner).wait_recv()
    for ys in range(4):
        fo[ys * 128:(ys + 1) * 128, :] = fout[:, ys].reshape(128, 128).astype(F32).T

VM = pl.BlockSpec(memory_space=pltpu.VMEM)
HBM = pl.BlockSpec(memory_space=pltpu.HBM)
DMA = pltpu.SemaphoreType.DMA


def sds(shape, dtype):
    return jax.ShapeDtypeStruct(shape, dtype)


def on_device(block_input, featurizer, filters, out_weight, grad_output):
    scale = 1.0 / math.sqrt(128 * lax.axis_size("ctx"))
    gf, dw, gfilt = pl.pallas_call(
        functools.partial(block_kernel, scale),
        out_shape=(sds((3, 2, 2, 32, 512), BF), sds((64, 512), F32), sds((512, 128), F32)),
        in_specs=[HBM] * 5,
        out_specs=(VM, VM, VM),
        scratch_shapes=[
            pltpu.VMEM((4, 4, 32, 4096), BF),
            pltpu.VMEM((2, 4, 4, 4, 32, 512), BF),
            pltpu.VMEM((8, 4, 4, 2, 64, 128), BF),
            pltpu.VMEM((4, 64, 512), BF),
            pltpu.VMEM((128, 128), BF),
            pltpu.VMEM((128, 128), BF),
            pltpu.VMEM((512, 512), F32),
            pltpu.VMEM((4, 512, 128), BF),
            pltpu.VMEM((18, 2, 32, 128), BF),
            pltpu.VMEM((18, 2, 32, 128), BF),
            pltpu.VMEM((1152, 128), F32),
            pltpu.VMEM((1152, 128), F32),
            pltpu.VMEM((128, 128), F32),
            pltpu.VMEM((128, 8, 128), F32),
            pltpu.VMEM((8, 2, 8, 128), F32),
            pltpu.VMEM((128, 512), BF),
            pltpu.VMEM((8, 3, 2, 32, 128), BF),
            pltpu.VMEM((8, 128, 256), BF),
            pltpu.VMEM((8, 128, 256), F32),
            pltpu.VMEM((8, 128, 256), BF),
            pltpu.VMEM((7, 128, 256), BF),
            pltpu.VMEM((7, 128, 256), BF),
            pltpu.VMEM((4, 64, 128), F32),
            pltpu.VMEM((16, 8, 128), F32),
            pltpu.VMEM((8, 128), F32),
            pltpu.VMEM((4, 2, 8, 128), F32),
            pltpu.VMEM((4, 16, 128), BF),
            pltpu.VMEM((8, 4, 16, 128), BF),
            DMA((120,)), DMA((120,)), DMA((28,)), DMA((28,)), DMA((7,)), DMA((7,)), DMA((8,)), DMA((8,)),
            DMA((8,)), DMA((8,)), DMA((7,)), DMA((7,)), DMA((4,)), DMA((4,)), DMA((32,)), DMA((32,)),
            DMA((16,)),
        ],
        compiler_params=pltpu.CompilerParams(
            collective_id=1, has_side_effects=True, vmem_limit_bytes=60 * 2**20
        ),
        name="hyena_block",
    )(block_input, grad_output, featurizer.transpose(1, 0, 2), out_weight, filters)
    return gf.reshape(3, 128, 512).transpose(1, 0, 2), dw, gfilt


def solution(mesh):
    placed = (
        P(("ctx", "tp"), None),
        P("ctx", None, "tp"),
        P("tp", None),
        P("ctx", "tp"),
        P(("ctx", "tp"), None),
    )
    return jax.shard_map(
        on_device,
        mesh=mesh,
        in_specs=placed,
        out_specs=(P("ctx", None, "tp"), P("ctx", "tp"), P("tp", None)),
        check_vma=False,
    )
```

```python
import functools
import math

import jax
import jax.numpy as jnp
from jax import lax
from jax.experimental import pallas as pl
from jax.experimental.pallas import tpu as pltpu
from jax.sharding import PartitionSpec as P

MESH = pl.DeviceIdType.MESH
BF = jnp.bfloat16
F32 = jnp.float32
FP, FM, HP, HM = 0, 1, 2, 3
FAR = ((4, 3, 5, 2), (6, 1, 7, 0))


def coords():
    ctx = lax.axis_index("ctx")
    tp = lax.axis_index("tp")
    z = ctx // 8
    y = (ctx // 2) % 4
    xl = ctx % 2
    xh = tp // 2
    core = tp % 2
    return xh, xl, y, z, core


def dev(xh, xl, y, z, core):
    return ((z * 4 + y) * 2 + xl, xh * 2 + core)


def devx(x, y, z, core):
    return dev(x // 2, x % 2, y, z, core)


def slot_of(x):
    return (x % 2) * 2 + x // 2


def remote(src, dst, ssem, rsem, device):
    return pltpu.make_async_remote_copy(
        src_ref=src, dst_ref=dst, send_sem=ssem, recv_sem=rsem, device_id=device, device_id_type=MESH
    )


class Plane:
    def __init__(self, place, ssem, rsem, base, here):
        self.place, self.ssem, self.rsem, self.base = place, ssem, rsem, base
        self.x, self.y, self.z, self.core = here
        self.sent = []

    def unit(self, lr, a, b, half):
        dx, dy = (a, b) if lr == 0 else (b, a)
        return self.place((self.y + dy) % 4, slot_of((self.x + dx) % 4), lr, half)

    def neighbour(self, lr, axis, by):
        if (lr == 0) == (axis == 0):
            return devx((self.x + by) % 4, self.y, self.z, self.core)
        return devx(self.x, (self.y + by) % 4, self.z, self.core)

    def sem(self, lr, axis, a, kind):
        return self.base + lr * 20 + (kind if axis == 0 else 4 + a * 4 + kind)

    def send(self, lr, axis, a, kind):
        by = 1 if kind in (FP, HP) else 3
        back = {FP: 0, FM: 0, HP: 3, HM: 1}[kind]
        half = {FP: None, FM: None, HP: 0, HM: 1}[kind]
        place = (back, 0) if axis == 0 else (a, back)
        ref = self.unit(lr, place[0], place[1], half)
        s = self.sem(lr, axis, a, kind)
        copy = remote(ref, ref, self.ssem.at[s], self.rsem.at[s], self.neighbour(lr, axis, by))
        copy.start()
        self.sent.append(copy)

    def wait(self, lr, axis, a, kind):
        off = {FP: 3, FM: 1, HP: 2, HM: 2}[kind]
        half = {FP: None, FM: None, HP: 0, HM: 1}[kind]
        place = (off, 0) if axis == 0 else (a, off)
        dst = self.unit(lr, place[0], place[1], half)
        s = self.sem(lr, axis, a, kind)
        remote(dst, dst, self.ssem.at[s], self.rsem.at[s], self.neighbour(lr, axis, 1)).wait_recv()

    def step1(self):
        for axis in range(2):
            for lr in range(2):
                for kind in (FP, FM):
                    self.send(lr, axis, 0, kind)

    def step2(self):
        for kind, a, hkind in ((FP, 3, HP), (FM, 1, HM)):
            for lr in range(2):
                self.wait(lr, 0, 0, kind)
                self.send(lr, 0, 0, hkind)
                self.send(lr, 1, a, FP)
                self.send(lr, 1, a, FM)

    def step3(self):
        for lr in range(2):
            self.wait(lr, 0, 0, HP)
            self.wait(lr, 0, 0, HM)
            self.send(lr, 1, 2, FP)
            self.send(lr, 1, 2, FM)

    def step4(self, a):
        for kind, hkind in ((FP, HP), (FM, HM)):
            for lr in range(2):
                self.wait(lr, 1, a, kind)
                self.send(lr, 1, a, hkind)

    def step5(self):
        for a in (0, 3, 1, 2):
            for lr in range(2):
                self.wait(lr, 1, a, HP)
                self.wait(lr, 1, a, HM)

    def finish(self):
        for copy in self.sent:
            copy.wait_send()


def block_kernel(
    scale,
    x_ref, g_ref, f_ref, w_ref, filt_ref,
    gfo, dw_out, fo,
    xbuf, gbuf, wbuf, wst, fst, filt_recv, acc, qkvg, gext, mext, gx, mx, taps, corr_acc, corr, mo,
    gfb, dsend_buf, down, pbuf, sbuf, zbuf, tbuf, fz, ftot, fin, finb, fout,
    psend, precv, wsend, wrecv, hsend, hrecv, gsend, grecv, dsend, drecv, asend, arecv, osend, orecv, fsend, frecv,
    lsem,
):
    xh, xl, y, z, core = coords()
    x = xh * 2 + xl
    here = (x, y, z, core)
    other = 1 - core
    zp, zm = (z + 1) % 8, (z + 7) % 8
    partner = dev(xh, xl, y, z, other)
    same = xl == core
    apart = jnp.logical_not(same)
    me_slot = slot_of(x)

    barrier = pltpu.get_barrier_semaphore()
    greet = [
        devx((x + 1) % 4, y, z, core), devx((x + 3) % 4, y, z, core),
        devx(x, (y + 1) % 4, z, core), devx(x, (y + 3) % 4, z, core),
        partner,
        dev(xh, 1 - xl, y, z, other),
    ] + [dev(xh, core, (y + dy) % 4, z, xl) for dy in (1, 2, 3)]
    greet += [devx(x, y, zp, core), devx(x, y, zm, core)]
    for d in greet:
        pl.semaphore_signal(barrier, inc=1, device_id=d, device_id_type=MESH)
    stage = [
        pltpu.make_async_copy(f_ref, wst.at[pl.ds(0, 3)], lsem.at[0]),
        pltpu.make_async_copy(w_ref, wst.at[3], lsem.at[1]),
        pltpu.make_async_copy(x_ref, xbuf.at[y, me_slot], lsem.at[2]),
        pltpu.make_async_copy(filt_ref.at[pl.ds(pl.multiple_of(y * 128, 128), 128)], fst, lsem.at[3]),
    ]
    for h in range(2):
        for k in range(4):
            zz = (z + FAR[h][k]) % 8
            stage.append(pltpu.make_async_copy(
                g_ref.at[:, pl.ds(pl.multiple_of(zz * 512, 512), 512)], gbuf.at[h, y, me_slot, k], lsem.at[4 + h * 4 + k]
            ))
    for c in stage:
        c.start()
    for c in stage:
        c.wait()
    pl.semaphore_wait(barrier, len(greet))

    def place_x(yy, s, lr, half):
        cols = pl.ds(0, 4096) if half is None else pl.ds(half * 2048, 2048)
        return xbuf.at[yy, s, pl.ds(lr * 16, 16), cols]

    def place_g(h):
        def place(yy, s, lr, half):
            ks = pl.ds(0, 4) if half is None else pl.ds(half * 2, 2)
            return gbuf.at[h, yy, s, ks, pl.ds(lr * 16, 16), :]
        return place

    xs = Plane(place_x, psend, precv, 0, here)
    ga = Plane(place_g(0), psend, precv, 40, here)
    gb = Plane(place_g(1), psend, precv, 80, here)
    sent = []

    def start(c):
        c.start()
        sent.append(c)

    def wslice(yy):
        return wst.at[:, :, pl.ds(pl.multiple_of(yy * 128, 128), 128)]

    for dy in (1, 2, 3):
        yy = (y + dy) % 4
        start(remote(wslice(yy), wbuf.at[z, :, y, xl], wsend.at[dy], wrecv.at[dy], dev(xh, core, yy, z, xl)))
    own_local = pltpu.make_async_copy(wslice(y), wbuf.at[z, :, y, core], lsem.at[12])
    own_remote = remote(
        wslice(y), wbuf.at[z, :, y, xl], wsend.at[0], wrecv.at[0], dev(xh, 1 - xl, y, z, other)
    )

    @pl.when(same)
    def _():
        own_local.start()

    @pl.when(apart)
    def _():
        own_remote.start()

    xs.step1()
    filt_copy = remote(fst, filt_recv, hsend.at[0], hrecv.at[0], partner)
    start(filt_copy)

    def wblock(zrel, kinds=None, e=None):
        e = core if e is None else e
        zz = (z + 8 - zrel) % 8
        return wbuf.at[zz, :, :, e] if kinds is None else wbuf.at[zz, pl.ds(kinds, 2), :, e]

    def wring_send(plus, hop, piece):
        blk = wblock(hop - 1 if plus else (9 - hop) % 8, piece * 2)
        n = 4 + (0 if plus else 8) + (hop - 1) * 2 + piece
        start(remote(blk, blk, wsend.at[n], wrecv.at[n], devx(x, y, zp if plus else zm, core)))

    def wring_wait(plus, hop, piece):
        blk = wblock(hop if plus else 8 - hop, piece * 2)
        n = 4 + (0 if plus else 8) + (hop - 1) * 2 + piece
        remote(blk, blk, wsend.at[n], wrecv.at[n], devx(x, y, zp, core)).wait_recv()

    def wpair_send(zrel):
        blk = wblock(zrel)
        start(remote(blk, blk, wsend.at[20 + zrel], wrecv.at[20 + zrel], partner))

    def wpair_wait(zrel):
        blk = wblock(zrel, None, other)
        remote(blk, blk, wsend.at[20 + zrel], wrecv.at[20 + zrel], partner).wait_recv()

    def weights_in():
        @pl.when(same)
        def _():
            own_local.wait()

        @pl.when(apart)
        def _():
            blk = wbuf.at[z, :, y, core]
            own_remote.wait_send()
            remote(blk, blk, wsend.at[0], wrecv.at[0], dev(xh, 1 - xl, y, z, other)).wait_recv()

        for dy in (1, 2, 3):
            blk = wbuf.at[z, :, (y + 4 - dy) % 4, core]
            remote(blk, blk, wsend.at[dy], wrecv.at[dy], partner).wait_recv()
        for piece in range(2):
            wring_send(True, 1, piece)
            wring_send(False, 1, piece)
        wpair_send(0)

    def weights_hop(n):
        for piece in range(2):
            for plus in (True, False):
                if n < 4 or plus == (piece == 0):
                    wring_wait(plus, n, piece)
                    if n < 3 or (n == 3 and plus == (piece == 0)):
                        wring_send(plus, n + 1, piece)
        wpair_send(n)
        if n < 4:
            wpair_send(8 - n)

    xs.step2()
    xs.step4(0)
    weights_in()
    xs.step3()
    ga.step1()
    xs.step4(3)
    weights_hop(1)
    xs.step4(1)
    weights_hop(2)
    xs.step4(2)
    ga.step2()
    weights_hop(3)
    ga.step4(0)
    xs.step5()
    ga.step3()
    gb.step1()

    def project_x(zrels, fresh=False):
        total = None if fresh else acc[:, 0:384]
        for zrel in zrels:
            wpair_wait(zrel)
            i = (z + 8 - zrel) % 8
            cols = pl.ds(pl.multiple_of(i * 512, 512), 512)
            lhs = xbuf[:, :, :, cols].reshape(512, 512)
            rhs = jnp.concatenate([wbuf[i, kind].reshape(512, 128) for kind in range(3)], axis=1)
            term = jnp.dot(lhs, rhs, preferred_element_type=F32)
            total = term if total is None else total + term
        acc[:, 0:384] = total

    project_x((0, 1, 7), True)
    weights_hop(4)
    project_x((2, 6))
    ga.step4(3)
    project_x((3, 5, 4))

    for i in range(3):
        qkvg[i] = acc[:, i * 128:(i + 1) * 128].astype(BF)
    gated = (qkvg[1].astype(F32) * qkvg[2].astype(F32)).astype(BF)
    gext[pl.ds(2, 16), core] = gated.reshape(16, 32, 128)

    own = gext.at[pl.ds(2, 16), core]
    tail = gext.at[pl.ds(16, 2), core]
    head = gext.at[pl.ds(0, 2), core]
    start(remote(own, own, hsend.at[1], hrecv.at[1], partner))
    start(remote(tail, head, hsend.at[2], hrecv.at[2], devx(x, y, zp, core)))
    start(remote(tail, head, hsend.at[3], hrecv.at[3], devx(x, y, zp, other)))
    ga.step4(1)
    gb.step2()
    ga.step4(2)
    gb.step4(0)
    xs.finish()

    def project_g(h, k):
        lhs = gbuf[h, :, :, k].reshape(512, 512)
        rhs = wbuf[(z + FAR[h][k]) % 8, 3].reshape(512, 128)
        return jnp.dot(lhs, rhs, preferred_element_type=F32)

    filt_copy.wait_recv()
    mine = jnp.where(same, 1.0, 0.0)
    taps[...] = (fst[...].astype(F32) * mine + filt_recv[...].astype(F32) * (1.0 - mine)).T

    def hwait(i, blk):
        remote(blk, blk, hsend.at[i], hrecv.at[i], partner).wait_recv()

    hwait(1, gext.at[pl.ds(2, 16), other])
    hwait(2, gext.at[pl.ds(0, 2), core])
    hwait(3, gext.at[pl.ds(0, 2), other])
    first = jnp.where(z == 0, 0.0, 1.0)
    gx[0:128] = gext[0:2].reshape(128, 128).astype(F32) * first
    gx[128:1152] = gext[2:18].reshape(1024, 128).astype(F32)

    zero = jnp.zeros((32, 128), F32)

    def rows_of(i):
        lo = pl.multiple_of(i * 64, 64)
        return pl.ds(lo, 32), pl.ds(lo + 32, 32), pl.multiple_of((i * 4 + core) * 32, 32)

    def mixed_pair(i, _):
        r0, r1, base = rows_of(i)

        def taps8(jo, carry):
            m0, m1 = carry
            j0 = pl.multiple_of(jo * 8, 8)
            tap = taps[pl.ds(j0, 8), :]
            for ji in range(8):
                f = tap[ji:ji + 1, :]
                m0 = m0 + f * gx[pl.ds(base + 128 - j0 - ji, 32), :]
                m1 = m1 + f * gx[pl.ds(base + 192 - j0 - ji, 32), :]
            return m0, m1

        m0, m1 = lax.fori_loop(0, 16, taps8, (zero, zero))
        acc[r0, 0:128] = m0
        acc[r1, 0:128] = m1
        return 0

    lax.fori_loop(0, 4, mixed_pair, 0)
    gb.step3()
    lax.fori_loop(4, 8, mixed_pair, 0)
    mo[...] = (qkvg[0].astype(F32) * acc[:, 0:128]).T.astype(BF)
    ga.step5()
    gb.step4(3)

    def grad_w(h, k):
        def term(e):
            cols = pl.ds(pl.multiple_of(e * 256, 256), 256)
            rhs = gbuf[h, :, :, k, :, cols].reshape(512, 256)
            return jnp.dot(mo[...], rhs, preferred_element_type=F32)

        i = h * 4 + k
        dsend_buf[i] = term(other).astype(BF)
        start(remote(dsend_buf.at[i], pbuf.at[i], dsend.at[i], drecv.at[i], partner))
        down[i] = term(core)

    def both_cores(h, k):
        i, r = h * 4 + k, FAR[h][k]
        remote(pbuf.at[i], pbuf.at[i], dsend.at[i], drecv.at[i], partner).wait_recv()
        down[i] = down[i] + pbuf[i].astype(F32)
        if r:
            sbuf[i] = down[i].astype(BF)
            start(remote(sbuf.at[i], zbuf.at[i], asend.at[i], arecv.at[i], devx(x, y, (z + r) % 8, core)))

    for k in range(4):
        grad_w(0, k)
    gb.step4(1)
    for k in range(4):
        both_cores(0, k)
    gb.step4(2)
    acc[:, 384:512] = project_g(0, 0) + project_g(0, 1) + project_g(0, 2) + project_g(0, 3)
    ga.finish()
    gb.step5()
    acc[:, 384:512] += project_g(1, 0) + project_g(1, 1) + project_g(1, 2) + project_g(1, 3)

    qkvg[3] = acc[:, 384:512].astype(BF)
    gmixed = (qkvg[3].astype(F32) * qkvg[0].astype(F32)).astype(BF)
    mext[pl.ds(0, 16), core] = gmixed.reshape(16, 32, 128)
    mown = mext.at[pl.ds(0, 16), core]
    mhead = mext.at[pl.ds(0, 2), core]
    mtail = mext.at[pl.ds(16, 2), core]
    start(remote(mown, mown, hsend.at[4], hrecv.at[4], partner))
    start(remote(mhead, mtail, hsend.at[5], hrecv.at[5], devx(x, y, zm, core)))
    start(remote(mhead, mtail, hsend.at[6], hrecv.at[6], devx(x, y, zm, other)))

    corr_acc[...] = jnp.zeros_like(corr_acc)

    def corr_pair(i, _):
        _, _, base = rows_of(i)
        c0 = mext[pl.ds(i * 2, 1), core].reshape(32, 128).astype(F32)
        c1 = mext[pl.ds(i * 2 + 1, 1), core].reshape(32, 128).astype(F32)

        def taps8(jo, _):
            j0 = pl.multiple_of(jo * 8, 8)
            for ji in range(8):
                p = c0 * gx[pl.ds(base + 128 - j0 - ji, 32), :] + c1 * gx[pl.ds(base + 192 - j0 - ji, 32), :]
                corr_acc[j0 + ji] += (p[0:8] + p[8:16]) + (p[16:24] + p[24:32])
            return 0

        lax.fori_loop(0, 16, taps8, 0)
        return 0

    lax.fori_loop(0, 8, corr_pair, 0)
    corr[...] = jnp.sum(corr_acc[...], axis=1).reshape(8, 2, 8, 128)
    for r in range(8):
        zz = (z + r) % 8
        for e in range(2):
            if r == 0 and e == 0:
                continue
            to = core if e == 0 else other
            s = r * 2 + e
            start(remote(corr.at[zz, to], fz.at[s], fsend.at[s], frecv.at[s], devx(x, y, zz, to)))
    for k in range(4):
        grad_w(1, k)
    for k in range(4):
        both_cores(1, k)

    hwait(4, mext.at[pl.ds(0, 16), other])
    hwait(5, mext.at[pl.ds(16, 2), core])
    hwait(6, mext.at[pl.ds(16, 2), other])
    mx[0:1024] = mext[0:16].reshape(1024, 128).astype(F32)
    last = jnp.where(z == 7, 0.0, 1.0)
    mx[1024:1152] = mext[16:18].reshape(128, 128).astype(F32) * last

    def back_pair(i, _):
        r0, r1, base = rows_of(i)

        def taps8(jo, carry):
            m0, m1 = carry
            j0 = pl.multiple_of(jo * 8, 8)
            tap = taps[pl.ds(j0, 8), :]
            for ji in range(8):
                f = tap[ji:ji + 1, :]
                m0 = m0 + f * mx[pl.ds(base + j0 + ji, 32), :]
                m1 = m1 + f * mx[pl.ds(base + 64 + j0 + ji, 32), :]
            return m0, m1

        both = lax.fori_loop(0, 16, taps8, (zero, zero))
        for n, rows in enumerate((r0, r1)):
            gfb[i, 0, n] = (qkvg[3, rows, :].astype(F32) * acc[rows, 0:128]).astype(BF)
            gfb[i, 1, n] = (both[n] * qkvg[2, rows, :].astype(F32)).astype(BF)
            gfb[i, 2, n] = (both[n] * qkvg[1, rows, :].astype(F32)).astype(BF)
        return 0

    def gf_place(ysrc, csrc):
        return gfo.at[:, :, csrc, :, pl.ds(pl.multiple_of(ysrc * 128, 128), 128)]

    def gf_copy(i):
        return remote(
            gfb.at[i], gf_place(y, core), gsend.at[i], grecv.at[y * 2 + core], dev(xh, i % 2, i // 2, z, xl)
        )

    def gf_self(i):
        return jnp.logical_and(same, jnp.logical_and(y == i // 2, xl == i % 2))

    fin_local = pltpu.make_async_copy(ftot, fin.at[y, core], lsem.at[14])

    def f_copy(i):
        return remote(
            ftot, fin.at[y, core], fsend.at[16 + i], frecv.at[16 + y * 2 + core], dev(xh, i % 2, i // 2, z, xl)
        )

    def filters_out():
        fs = corr[z, core]
        for s in range(1, 16):
            remote(fz.at[s], fz.at[s], fsend.at[s], frecv.at[s], partner).wait_recv()
            fs = fs + fz[s]
        ftot[...] = fs * scale

        @pl.when(same)
        def _():
            fin_local.start()

        for i in range(8):
            @pl.when(jnp.logical_not(gf_self(i)))
            def _():
                f_copy(i).start()

    gf_local = pltpu.make_async_copy(gfb.at[y * 2 + xl], gf_place(y, core), lsem.at[13])
    for i in range(0, 8, 2):
        if i == 2:
            filters_out()
        lax.fori_loop(i, i + 2, back_pair, 0)
        for n in (i, i + 1):
            @pl.when(gf_self(n))
            def _():
                gf_local.start()

            @pl.when(jnp.logical_not(gf_self(n)))
            def _():
                gf_copy(n).start()

    total = down[7]
    for i in range(7):
        remote(zbuf.at[i], zbuf.at[i], asend.at[i], arecv.at[i], partner).wait_recv()
        total = total + zbuf[i].astype(F32)
    tbuf[...] = (total.T * scale).reshape(4, 64, 128)

    def dw_place(ysrc):
        return dw_out.at[:, pl.ds(pl.multiple_of(ysrc * 128, 128), 128)]

    def dw_copy(k):
        yp, xp = core * 2 + k // 2, k % 2
        return remote(tbuf.at[k], dw_place(y), osend.at[k], orecv.at[y], dev(xh, xp, yp, z, xl))

    dw_here = jnp.logical_and(same, y // 2 == core)

    def dw_self(k):
        return jnp.logical_and(dw_here, jnp.logical_and(y % 2 == k // 2, xl == k % 2))

    dw_local = pltpu.make_async_copy(tbuf.at[(y % 2) * 2 + xl], dw_place(y), lsem.at[15])

    @pl.when(dw_here)
    def _():
        dw_local.start()

    for k in range(4):
        @pl.when(jnp.logical_not(dw_self(k)))
        def _():
            dw_copy(k).start()

    @pl.when(same)
    def _():
        fin_local.wait()

    for ys in range(4):
        for cs in range(2):
            me = jnp.logical_and(same, jnp.logical_and(y == ys, core == cs))

            @pl.when(jnp.logical_not(me))
            def _():
                s = 16 + ys * 2 + cs
                blk = fin.at[ys, cs]
                remote(blk, blk, fsend.at[s], frecv.at[s], partner).wait_recv()
    finb[...] = fin[...].reshape(4, 16, 128).astype(BF)
    for r in range(1, 8):
        start(remote(finb, fout.at[z], fsend.at[24 + r], frecv.at[24 + r], devx(x, y, (z + r) % 8, core)))
    fout[z] = finb[...]

    @pl.when(dw_here)
    def _():
        dw_local.wait()

    for ys in range(4):
        @pl.when(jnp.logical_not(jnp.logical_and(dw_here, y == ys)))
        def _():
            blk = dw_place(ys)
            remote(blk, blk, osend.at[ys], orecv.at[ys], partner).wait_recv()

    @pl.when(same)
    def _():
        gf_local.wait()

    for ys in range(4):
        for cs in range(2):
            me = jnp.logical_and(same, jnp.logical_and(y == ys, core == cs))

            @pl.when(jnp.logical_not(me))
            def _():
                blk = gf_place(ys, cs)
                remote(blk, blk, gsend.at[0], grecv.at[ys * 2 + cs], partner).wait_recv()

    gb.finish()
    for c in sent:
        c.wait_send()
    for i in range(8):
        @pl.when(jnp.logical_not(gf_self(i)))
        def _():
            gf_copy(i).wait_send()
            f_copy(i).wait_send()
    for k in range(4):
        @pl.when(jnp.logical_not(dw_self(k)))
        def _():
            dw_copy(k).wait_send()

    for r in range(1, 8):
        blk = fout.at[(z + 8 - r) % 8]
        remote(blk, blk, fsend.at[24 + r], frecv.at[24 + r], partner).wait_recv()
    for ys in range(4):
        fo[ys * 128:(ys + 1) * 128, :] = fout[:, ys].reshape(128, 128).astype(F32).T

VM = pl.BlockSpec(memory_space=pltpu.VMEM)
HBM = pl.BlockSpec(memory_space=pltpu.HBM)
DMA = pltpu.SemaphoreType.DMA


def sds(shape, dtype):
    return jax.ShapeDtypeStruct(shape, dtype)


def on_device(block_input, featurizer, filters, out_weight, grad_output):
    scale = 1.0 / math.sqrt(128 * lax.axis_size("ctx"))
    gf, dw, gfilt = pl.pallas_call(
        functools.partial(block_kernel, scale),
        out_shape=(sds((3, 2, 2, 32, 512), BF), sds((64, 512), F32), sds((512, 128), F32)),
        in_specs=[HBM] * 5,
        out_specs=(VM, VM, VM),
        scratch_shapes=[
            pltpu.VMEM((4, 4, 32, 4096), BF),
            pltpu.VMEM((2, 4, 4, 4, 32, 512), BF),
            pltpu.VMEM((8, 4, 4, 2, 64, 128), BF),
            pltpu.VMEM((4, 64, 512), BF),
            pltpu.VMEM((128, 128), BF),
            pltpu.VMEM((128, 128), BF),
            pltpu.VMEM((512, 512), F32),
            pltpu.VMEM((4, 512, 128), BF),
            pltpu.VMEM((18, 2, 32, 128), BF),
            pltpu.VMEM((18, 2, 32, 128), BF),
            pltpu.VMEM((1152, 128), F32),
            pltpu.VMEM((1152, 128), F32),
            pltpu.VMEM((128, 128), F32),
            pltpu.VMEM((128, 8, 128), F32),
            pltpu.VMEM((8, 2, 8, 128), F32),
            pltpu.VMEM((128, 512), BF),
            pltpu.VMEM((8, 3, 2, 32, 128), BF),
            pltpu.VMEM((8, 128, 256), BF),
            pltpu.VMEM((8, 128, 256), F32),
            pltpu.VMEM((8, 128, 256), BF),
            pltpu.VMEM((7, 128, 256), BF),
            pltpu.VMEM((7, 128, 256), BF),
            pltpu.VMEM((4, 64, 128), F32),
            pltpu.VMEM((16, 8, 128), F32),
            pltpu.VMEM((8, 128), F32),
            pltpu.VMEM((4, 2, 8, 128), F32),
            pltpu.VMEM((4, 16, 128), BF),
            pltpu.VMEM((8, 4, 16, 128), BF),
            DMA((120,)), DMA((120,)), DMA((28,)), DMA((28,)), DMA((7,)), DMA((7,)), DMA((8,)), DMA((8,)),
            DMA((8,)), DMA((8,)), DMA((7,)), DMA((7,)), DMA((4,)), DMA((4,)), DMA((32,)), DMA((32,)),
            DMA((16,)),
        ],
        compiler_params=pltpu.CompilerParams(
            collective_id=1, has_side_effects=True, vmem_limit_bytes=60 * 2**20
        ),
        name="hyena_block",
    )(block_input, grad_output, featurizer.transpose(1, 0, 2), out_weight, filters)
    return gf.reshape(3, 128, 512).transpose(1, 0, 2), dw, gfilt


def solution(mesh):
    placed = (
        P(("ctx", "tp"), None),
        P("ctx", None, "tp"),
        P("tp", None),
        P("ctx", "tp"),
        P(("ctx", "tp"), None),
    )
    return jax.shard_map(
        on_device,
        mesh=mesh,
        in_specs=placed,
        out_specs=(P("ctx", None, "tp"), P("ctx", "tp"), P("tp", None)),
        check_vma=False,
    )
```
